128 devices in a mesh: ex: 16 (over z, y), stk: 8 (over x, core).
Axes of the slice: x: 4, y: 4, z: 4, core: 2. Of those that a mesh axis runs over, the one named last changes fastest.
Arguments:
- embeddings: bfloat16 [4096, 4096], P(None, 'ex'), may hold values from -6 to 6
- sign_bits: int32 [16, 4096], P('stk'), may hold values from 0 to 1
- permutation: int32 [16, 4096], P('stk'), may hold values from 0 to 4095, each once within a row
- gaussian: float32 [16, 4096], P('stk'), may hold values from -6 to 6
- scaling: float32 [16, 4096], P('stk'), may hold values from 0.5 to 2
- phases: float32 [16, 4096], P('stk'), may hold values from -3.140625 to 3.140625
- solution: float32 [64, 16, 4096], P(None, 'stk', 'ex'), may hold values from -6 to 6
- residual: float32 [64, 16, 4096], P(None, 'stk', 'ex'), may hold values from -240 to 240
- direction: float32 [64, 16, 4096], P(None, 'stk', 'ex'), may hold values from -240 to 240
Outputs:
- solution_following: float32 [64, 16, 4096], P(None, 'stk', 'ex')
- residual_next: float32 [64, 16, 4096], P(None, 'stk', 'ex')
- direction_following: float32 [64, 16, 4096], P(None, 'stk', 'ex')
The draws below stay inside these ranges and needn't reach their ends.
Inputs may be any that keep to these rules, and one draw needn't show every extreme that they name: `permutation`: each row holds every index of 0 to 4095 once.
All inputs are finite; a program needn't handle non-finite values.
Results may differ from the reference program's by a relative error of at most 0.0003.
Values sent between devices are 32-bit elements; how exact they have to be, the bound alone decides.
A program may use at most 128 MiB of HBM per device.

```python
import math
from functools import partial
import jax
import jax.numpy as jnp
from jax import lax

D = 4096
SIDE = 64
TARGETS = 64
STACKS = 16
EXAMPLES = 4096


def scaled_vector(key, noise, base):
    key_feature_draw, key_target = jax.random.split(key)
    feat_scale = jnp.exp(jax.random.uniform(key_feature_draw, (1, STACKS, D), jnp.float32) * math.log(10.0)) / math.sqrt(10.0)
    target_scale = jnp.exp(jax.random.uniform(key_target, (TARGETS, 1, 1), jnp.float32) * math.log(10.0)) / math.sqrt(10.0)
    stack_pos = jnp.arange(STACKS, dtype=jnp.float32)[None, :, None] / max(STACKS - 1, 1)
    column_offset = jnp.arange(D, dtype=jnp.float32)[None, None, :] / (D - 1)
    trend = base ** (stack_pos + column_offset) / base
    return noise * feat_scale * target_scale * trend


def draw_residual(key, part):
    key = jax.random.fold_in(key, 11)
    key_noise = jax.random.fold_in(key, 0)
    key_rest = jax.random.fold_in(key, 2)
    noise = jnp.clip(jax.random.normal(key_noise, (TARGETS, STACKS, D), jnp.float32), -4.0, 4.0)
    return scaled_vector(key_rest, noise, 3.0)


def draw_direction(key, part):
    key = jax.random.fold_in(key, 23)
    key_noise = jax.random.fold_in(key, 0)
    key_rest = jax.random.fold_in(key, 2)
    noise = jnp.clip(jax.random.normal(key_noise, (TARGETS, STACKS, D), jnp.float32), -4.0, 4.0)
    return scaled_vector(key_rest, noise, 3.0)


def with_ends(values, own_key, low, high):
    longest = values.shape.index(max(values.shape))
    spots = []
    for shift in (0, 1):
        where = [jax.random.randint(jax.random.fold_in(own_key, axis), (), 0, length) for axis, length in enumerate(values.shape)]
        where[longest] = (where[longest] + shift) % values.shape[longest]
        spots.append(tuple(where))
    return values.at[spots[0]].set(low).at[spots[1]].set(high)


def block_scale(stream_key, extent, cuts, low, high):
    def one(position, parts):
        steps = jax.random.uniform(jax.random.fold_in(jax.random.fold_in(stream_key, 6), position), (parts,), jnp.float32, low / len(cuts), high / len(cuts))
        return jnp.repeat(jnp.exp(steps), extent[position] // parts).reshape((-1,) + (1,) * (len(extent) - position - 1))

    level = one(*cuts[0])
    for cut in cuts[1:]:
        level = level * one(*cut)
    return level


def centred(key, shape, scale, most, pieces=(), kind=jnp.bfloat16):
    result = scale * jax.random.normal(key, shape, jnp.float32)
    if pieces:
        result = result * block_scale(key, shape, pieces, -0.22, 0.18)
    return jnp.clip(result, -most, most).astype(kind)


def setup_inputs(seed: int = 0) -> dict:
    key_of = jax.random.split(jax.random.key(seed), 10)
    return {
        "embeddings": centred(key_of[0], (D, EXAMPLES), 1.0, 6.0, ((1, 16),)),
        "sign_bits": with_ends(jax.random.randint(key_of[1], (STACKS, D), 0, 2), jax.random.fold_in(key_of[1], 1), 0, 1).astype(jnp.int32),
        "permutation": jax.vmap(lambda own: jax.random.permutation(own, D))(jax.random.split(key_of[2], STACKS)).reshape((STACKS, D)).astype(jnp.int32),
        "gaussian": centred(key_of[3], (STACKS, D), 1.0, 6.0, ((0, 8),), jnp.float32),
        "scaling": jnp.clip(jnp.exp(math.log(2.0) - 1.3862944 * jax.random.uniform(key_of[4], (STACKS, D), jnp.float32) ** block_scale(key_of[4], (STACKS, D), ((0, 8),), -0.2, 0.2)), 0.5, 2.0),
        "phases": jnp.clip(jax.random.uniform(key_of[5], (STACKS, D), jnp.float32, -3.140625, 3.140625), -3.140625, 3.140625),
        "solution": centred(key_of[6], (TARGETS, STACKS, D), 1.0, 6.0, ((1, 8), (2, 16)), jnp.float32),
        "residual": draw_residual(jax.random.fold_in(key_of[9], 71), 0),
        "direction": draw_direction(jax.random.fold_in(key_of[9], 71), 0),
    }


ridge = 0.25
epsilon = 1e-06

def parity_table(edge_size):
    counter = jnp.arange(edge_size, dtype=jnp.int32)
    common = jnp.zeros((edge_size, edge_size), jnp.int32)
    for bit_level in range(max(edge_size.bit_length() - 1, 1)):
        bit_vals = counter // 2 ** bit_level % 2
        common = common + bit_vals[:, None] * bit_vals[None, :]
    return (1 - 2 * (common % 2)).astype(jnp.float32)

def transform(field, walsh_hadamard_transform):
    edge_size = walsh_hadamard_transform.shape[0]
    columns = field.shape[1]
    blocked_layout = field.reshape(edge_size, edge_size, columns)
    blocked_layout = jnp.einsum('ev,vtq->etq', walsh_hadamard_transform, blocked_layout, precision=lax.Precision.HIGHEST)
    blocked_layout = jnp.einsum('aq,zqx->zax', walsh_hadamard_transform, blocked_layout, precision=lax.Precision.HIGHEST)
    return blocked_layout.reshape(edge_size * edge_size, columns)

def stack_panel(data, walsh_hadamard_transform, weight_norm, sign_row, perm_row, gauss_row, scale_row, phase_row):
    signed = data * (2 * sign_row - 1).astype(jnp.float32)[:, None]
    spread_row_block = transform(signed, walsh_hadamard_transform)
    shuffled = jnp.take(spread_row_block, perm_row.astype(jnp.int32), axis=0) * gauss_row[:, None]
    angles = scale_row[:, None] * transform(shuffled, walsh_hadamard_transform) / data.shape[0] + phase_row[:, None]
    return weight_norm * jnp.cos(angles)

def reference(embeddings, sign_bits, permutation, gaussian, scaling, phases, solution, residual, direction):
    data = embeddings.astype(jnp.float32)
    walsh_hadamard_transform = parity_table(SIDE)
    weight_norm = math.sqrt(2.0 / (STACKS * D))
    build = partial(stack_panel, data, walsh_hadamard_transform, weight_norm)
    stack_dirs = jnp.moveaxis(direction, 1, 0)

    def accumulate(carry, params):
        panel = build(params[0], params[1], params[2], params[3], params[4])
        return (carry + jnp.einsum('tj,jn->tn', params[5], panel, precision=lax.Precision.HIGHEST), None)
    start = jnp.zeros((TARGETS, data.shape[1]), jnp.float32)
    projected = lax.scan(accumulate, start, (sign_bits, permutation, gaussian, scaling, phases, stack_dirs))[0]

    def apply_stack(params):
        panel = build(params[0], params[1], params[2], params[3], params[4])
        return jnp.einsum('tn,jn->tj', projected, panel, precision=lax.Precision.HIGHEST)
    summed = lax.map(apply_stack, (sign_bits, permutation, gaussian, scaling, phases))
    applied = ridge * direction + jnp.moveaxis(summed, 0, 1)
    norm_old = lax.optimization_barrier(jnp.sum(residual * residual, axis=(1, 2)))
    direction_curvature = lax.optimization_barrier(jnp.sum(direction * applied, axis=(1, 2)))
    step_size = (norm_old / direction_curvature)[:, None, None]
    solution_following = solution + step_size * direction
    residual_next = residual - step_size * applied
    norm_new = lax.optimization_barrier(jnp.sum(residual_next * residual_next, axis=(1, 2)))
    conjugacy = (norm_new / (norm_old + epsilon))[:, None, None]
    direction_following = residual_next + conjugacy * direction
    return (solution_following, residual_next, direction_following)
```

```python
import functools
import math

import jax
import jax.numpy as jnp
from jax import lax
from jax.experimental import pallas as pl
from jax.experimental.pallas import tpu as pltpu
from jax.sharding import PartitionSpec as P

f32, bf16 = jnp.float32, jnp.bfloat16
MESH = pl.DeviceIdType.MESH

D = 4096
BLK = 256
NB = 16
NS = 8
T = 64
RIDGE = 0.25
EPSILON = 1e-06
TURN = 1.0 / (2.0 * math.pi)
NORM = math.sqrt(2.0 / (16 * D))
SINE = (6.283164044251588, -41.337142364570006, 81.34076867837481, -70.99343135659183)
COEF = tuple(c * NORM for c in SINE)


def hadamard():
    i = lax.broadcasted_iota(jnp.int32, (BLK, BLK), 0)
    j = lax.broadcasted_iota(jnp.int32, (BLK, BLK), 1)
    v = i & j
    v = v ^ (v >> 4)
    v = v ^ (v >> 2)
    v = v ^ (v >> 1)
    return (1 - 2 * (v & 1)).astype(f32)


def butterfly(values):
    v = list(values)
    h = 1
    while h < len(v):
        for i in range(0, len(v), 2 * h):
            for k in range(i, i + h):
                v[k], v[k + h] = v[k] + v[k + h], v[k] - v[k + h]
        h *= 2
    return v


def split(x):
    hi = x.astype(bf16)
    return hi, (x - hi.astype(f32)).astype(bf16)


def dot(a, b):
    return jnp.dot(a, b, preferred_element_type=f32)


def dot_t(a, b):
    return lax.dot_general(a, b, (((1,), (1,)), ((), ())), preferred_element_type=f32)


def row_sums(x):
    ones = jnp.ones((8, x.shape[1]), f32)
    return lax.dot_general(
        ones, x, (((1,), (1,)), ((), ())), precision=lax.Precision.HIGHEST, preferred_element_type=f32
    )


def column(row):
    wide = jnp.concatenate([row, row], axis=1)
    return jnp.transpose(wide)[:T, 0:1]


def columns_of_parameters(gauss, scale, phase, col):
    for b in range(D // 128):
        at = slice(b * 128, (b + 1) * 128)
        block = jnp.concatenate(
            [
                gauss[:, at],
                scale[:, at] * (TURN / D),
                phase[:, at] * TURN,
                jnp.zeros((2, 128), f32),
            ],
            axis=0,
        )
        col[at, :] = jnp.transpose(block)


def spread_blocks(s, sign, emb, h, y):
    def body(a, _):
        o = pl.multiple_of(a * BLK, BLK)
        signs = (2 * sign[s : s + 1, pl.ds(o, BLK)] - 1).astype(f32)
        y[pl.ds(o, BLK), :] = dot((h * signs).astype(bf16), emb[pl.ds(o, BLK), :])
        return 0

    lax.fori_loop(0, NB, body, 0, unroll=4)


def spread_across(y, sp):
    def body(r, _):
        o = pl.multiple_of(r * 8, 8)
        for half in range(2):
            lanes = slice(half * 128, (half + 1) * 128)
            v = butterfly([y[pl.ds(a * BLK + o, 8), lanes] for a in range(NB)])
            for a in range(NB):
                sp[half, pl.ds(a * BLK + o, 8), :] = v[a]
        return 0

    lax.fori_loop(0, BLK // 8, body, 0)


def permute(perm, sp, y):
    groups = 8

    def body(jb, _):
        o = pl.multiple_of(jb * 8 * groups, 8 * groups)
        for q in range(groups):
            at = pl.multiple_of(o + q * 8, 8)
            rows = [y.at[pl.ds(at, 8), half * 128 : (half + 1) * 128] for half in range(2)]
            for k in range(8):
                idx = perm[o + q * 8 + k]
                for half in range(2):
                    rows[half][k : k + 1, :] = sp[half, pl.ds(idx, 1), :]
        return 0

    lax.fori_loop(0, D // (8 * groups), body, 0)


def mix_across(s, y, col, z):
    def body(r, _):
        o = pl.multiple_of(r * 16, 16)
        gauss = [jnp.broadcast_to(col[pl.ds(a * BLK + o, 16), s : s + 1], (16, 128)) for a in range(NB)]
        for half in range(2):
            lanes = slice(half * 128, (half + 1) * 128)
            v = butterfly([y[pl.ds(a * BLK + o, 16), lanes] * gauss[a] for a in range(NB)])
            for a in range(NB):
                hi, lo = split(v[a])
                z[a, pl.ds(o, 16), lanes] = hi
                z[a, pl.ds(BLK + o, 16), lanes] = lo
        return 0

    lax.fori_loop(0, BLK // 16, body, 0)


def cosine(turns):
    x = 0.25 - jnp.abs(turns - jnp.round(turns))
    u = x * x
    p = COEF[3]
    for c in COEF[2::-1]:
        p = p * u + c
    return p * x


def features(s, z, h2, col, fh, fl):
    def body(a, _):
        o = pl.multiple_of(a * BLK, BLK)
        scale = col[pl.ds(o, BLK), 2 + s : 3 + s]
        phase = col[pl.ds(o, BLK), 4 + s : 5 + s]
        hi, lo = split(cosine(dot(h2, z[a]) * scale + phase))
        fh[s, a] = hi
        fl[s, a] = lo
        return 0

    lax.fori_loop(0, NB, body, 0, unroll=2)


def kernel(
    emb, sign, perm_hbm, gauss, scale, phase, sol, res, dire,
    sol_out, res_out, dir_out,
    perm0, perm1, y, sp, z, fh, fl, col,
    dall, stat, stat2, pacc, precv, pown, pfull, isend, irecv, pp, nn, nn2,
    perm_sem, d_send, d_recv, st_send, st_recv, st2_send, st2_recv,
    p1_send, p1_recv, p2_send, p2_recv, i_send, i_recv, pp_send, pp_recv,
    n1_send, n1_recv, n2_send, n2_recv,
):
    ex = lax.axis_index("ex")
    st = lax.axis_index("stk")
    ez, ey = ex // 4, ex % 4

    def ex_to(k):
        return ((ez + k // 4) % 4) * 4 + (ey + k % 4) % 4

    def ex_from(k):
        return ((ez + 4 - k // 4) % 4) * 4 + (ey + 4 - k % 4) % 4

    def st_to(k):
        return (st + k) % NS

    def st_from(k):
        return (st + NS - k) % NS

    def to_ex(k, src, dst, send, recv):
        return pltpu.make_async_remote_copy(
            src_ref=src, dst_ref=dst, send_sem=send.at[k], recv_sem=recv.at[k],
            device_id=(ex_to(k), st), device_id_type=MESH,
        )

    def to_st(k, src, dst, send, recv):
        return pltpu.make_async_remote_copy(
            src_ref=src, dst_ref=dst, send_sem=send.at[k], recv_sem=recv.at[k],
            device_id=(ex, st_to(k)), device_id_type=MESH,
        )

    def each(n, f):
        def body(k, _):
            f(k)
            return 0

        lax.fori_loop(1, n, body, 0)

    barrier = pltpu.get_barrier_semaphore()
    each(NB, lambda k: pl.semaphore_signal(barrier, inc=1, device_id=(ex_to(k), st), device_id_type=MESH))
    each(NS, lambda k: pl.semaphore_signal(barrier, inc=1, device_id=(ex, st_to(k)), device_id_type=MESH))
    perms = [perm0, perm1]
    perm_copies = [pltpu.make_async_copy(perm_hbm.at[s], perms[s], perm_sem.at[s]) for s in range(2)]
    for c in perm_copies:
        c.start()

    for s in range(2):
        dall[ex, s] = dire[:, s, :]
    r2 = row_sums(jnp.concatenate([jnp.square(res[:, s, :]) for s in range(2)], axis=1))
    d2 = row_sums(jnp.concatenate([jnp.square(dire[:, s, :]) for s in range(2)], axis=1))
    stat[0] = jnp.concatenate([r2, d2], axis=1)

    h = hadamard()
    hb = h.astype(bf16)
    h2 = jnp.concatenate([hb, hb], axis=1)
    columns_of_parameters(gauss, scale, phase, col)
    spread_blocks(0, sign, emb, h, y)

    pl.semaphore_wait(barrier, NB - 1 + NS - 1)

    def d_copy(k):
        return to_ex(k, dall.at[ex], dall.at[ex], d_send, d_recv)

    def st_copy(k):
        return to_ex(k, stat.at[0], stat.at[k], st_send, st_recv)

    each(NB, lambda k: st_copy(k).start())
    each(NB, lambda k: d_copy(k).start())

    spread_across(y, sp)
    perm_copies[0].wait()
    permute(perms[0], sp, y)
    mix_across(0, y, col, z)
    features(0, z, h2, col, fh, fl)

    each(NB, lambda k: st_copy(k).wait())
    stat2[0] = jnp.sum(stat[...], axis=0)

    def st2_copy(k):
        return to_st(k, stat2.at[0], stat2.at[k], st2_send, st2_recv)

    each(NS, lambda k: st2_copy(k).start())

    spread_blocks(1, sign, emb, h, y)
    spread_across(y, sp)
    perm_copies[1].wait()
    permute(perms[1], sp, y)
    mix_across(1, y, col, z)
    features(1, z, h2, col, fh, fl)

    each(NS, lambda k: st2_copy(k).wait())
    totals = jnp.sum(stat2[...], axis=0)
    norm_old, d_norm = totals[:, :T], totals[:, T:]

    def project(e):
        for s in range(2):
            hi, lo = split(dall[e, s])
            both = dot(jnp.concatenate([hi, lo], axis=0), fh[s, e])
            pacc[...] += both[:T] + both[T:] + dot(hi, fl[s, e])

    pacc[...] = jnp.zeros_like(pacc)
    project(ex)

    def arrived(k):
        d_copy(k).wait_recv()
        project(ex_from(k))

    each(NB, arrived)

    def rows(i):
        return pl.ds(pl.multiple_of(i * 8, 8), 8)

    def p1_copy(k):
        return to_st(k, pacc.at[rows(st_to(k))], precv.at[k], p1_send, p1_recv)

    each(NS, lambda k: p1_copy(k).start())
    precv[0] = pacc[rows(st), :]
    each(NS, lambda k: p1_copy(k).wait_recv())
    pown[...] = jnp.sum(precv[...], axis=0)

    def p2_copy(k):
        return to_st(k, pown, pfull.at[rows(st)], p2_send, p2_recv)

    each(NS, lambda k: p2_copy(k).start())
    pfull[rows(st), :] = pown[...]

    def p2_arrived(k):
        pltpu.make_async_remote_copy(
            src_ref=pown, dst_ref=pfull.at[rows(st_from(k))], send_sem=p2_send.at[k], recv_sem=p2_recv.at[k],
            device_id=(ex, st_to(k)), device_id_type=MESH,
        ).wait_recv()

    each(NS, p2_arrived)

    projected = pfull[...]
    p_hi, p_lo = split(projected)
    p_both = jnp.concatenate([p_hi, p_lo], axis=0)

    def image(e):
        for s in range(2):
            both = dot_t(p_both, fh[s, e])
            isend[e, s] = both[:T] + both[T:] + dot_t(p_hi, fl[s, e])

    def i_copy(k):
        return to_ex(k, isend.at[ex_to(k)], irecv.at[k], i_send, i_recv)

    def image_out(k):
        image(ex_to(k))
        i_copy(k).start()

    each(NB, image_out)
    image(ex)
    irecv[0] = isend[ex]

    pp_row = row_sums(jnp.square(projected))
    pp[0] = jnp.concatenate([pp_row, pp_row], axis=1)

    def pp_copy(k):
        return to_ex(k, pp.at[0], pp.at[k], pp_send, pp_recv)

    each(NB, lambda k: pp_copy(k).start())
    each(NB, lambda k: pp_copy(k).wait())
    p_norm = jnp.sum(pp[...], axis=0)[:, :T]
    step = column(norm_old / (RIDGE * d_norm + p_norm))

    for s in range(2):
        sol_out[:, s, :] = sol[:, s, :] + step * dire[:, s, :]

    each(NB, lambda k: i_copy(k).wait_recv())
    nexts = []
    for s in range(2):
        applied = RIDGE * dire[:, s, :] + jnp.sum(irecv[:, s], axis=0)
        nexts.append(res[:, s, :] - step * applied)
        res_out[:, s, :] = nexts[s]
    n_row = row_sums(jnp.concatenate([jnp.square(v) for v in nexts], axis=1))
    nn[0] = jnp.concatenate([n_row, n_row], axis=1)

    def n1_copy(k):
        return to_ex(k, nn.at[0], nn.at[k], n1_send, n1_recv)

    each(NB, lambda k: n1_copy(k).start())
    each(NB, lambda k: n1_copy(k).wait())
    nn2[0] = jnp.sum(nn[...], axis=0)

    def n2_copy(k):
        return to_st(k, nn2.at[0], nn2.at[k], n2_send, n2_recv)

    each(NS, lambda k: n2_copy(k).start())
    each(NS, lambda k: n2_copy(k).wait())
    norm_new = jnp.sum(nn2[...], axis=0)[:, :T]
    conjugacy = column(norm_new / (norm_old + EPSILON))
    for s in range(2):
        dir_out[:, s, :] = nexts[s] + conjugacy * dire[:, s, :]

    each(NB, lambda k: d_copy(k).wait_send())
    each(NB, lambda k: i_copy(k).wait_send())
    each(NS, lambda k: p1_copy(k).wait_send())
    each(NS, lambda k: p2_copy(k).wait_send())


def local(embeddings, sign_bits, permutation, gaussian, scaling, phases, solution, residual, direction):
    vmem = pl.BlockSpec(memory_space=pltpu.VMEM)
    shape = jax.ShapeDtypeStruct(direction.shape, f32)
    dma = pltpu.SemaphoreType.DMA
    return pl.pallas_call(
        kernel,
        out_shape=[shape] * 3,
        in_specs=[vmem, vmem, pl.BlockSpec(memory_space=pl.ANY)] + [vmem] * 6,
        out_specs=[vmem] * 3,
        scratch_shapes=[
            pltpu.SMEM((D,), jnp.int32),
            pltpu.SMEM((D,), jnp.int32),
            pltpu.VMEM((D, BLK), f32),
            pltpu.VMEM((2, D, 128), f32),
            pltpu.VMEM((NB, 2 * BLK, BLK), bf16),
            pltpu.VMEM((2, NB, BLK, BLK), bf16),
            pltpu.VMEM((2, NB, BLK, BLK), bf16),
            pltpu.VMEM((D, 8), f32),
            pltpu.VMEM((NB, 2, T, BLK), f32),
            pltpu.VMEM((NB, 8, 128), f32),
            pltpu.VMEM((NS, 8, 128), f32),
            pltpu.VMEM((T, BLK), f32),
            pltpu.VMEM((NS, 8, BLK), f32),
            pltpu.VMEM((8, BLK), f32),
            pltpu.VMEM((T, BLK), f32),
            pltpu.VMEM((NB, 2, T, BLK), f32),
            pltpu.VMEM((NB, 2, T, BLK), f32),
            pltpu.VMEM((NB, 8, 128), f32),
            pltpu.VMEM((NB, 8, 128), f32),
            pltpu.VMEM((NS, 8, 128), f32),
            dma((2,)),
            dma((NB,)), dma((NB,)), dma((NB,)), dma((NB,)), dma((NS,)), dma((NS,)),
            dma((NS,)), dma((NS,)), dma((NS,)), dma((NS,)), dma((NB,)), dma((NB,)), dma((NB,)), dma((NB,)),
            dma((NB,)), dma((NB,)), dma((NS,)), dma((NS,)),
        ],
        compiler_params=pltpu.CompilerParams(
            collective_id=0, has_side_effects=True, vmem_limit_bytes=52 * 2**20
        ),
    )(embeddings, sign_bits, permutation, gaussian, scaling, phases, solution, residual, direction)


def solution(mesh):
    rows, stacks, blocks = P(None, "ex"), P("stk", None), P(None, "stk", "ex")
    return jax.shard_map(
        local,
        mesh=mesh,
        in_specs=(rows, stacks, stacks, stacks, stacks, stacks, blocks, blocks, blocks),
        out_specs=(blocks, blocks, blocks),
        check_vma=False,
    )
```

```python
import functools
import math

import jax
import jax.numpy as jnp
from jax import lax
from jax.experimental import pallas as pl
from jax.experimental.pallas import tpu as pltpu
from jax.sharding import PartitionSpec as P

f32, bf16 = jnp.float32, jnp.bfloat16
MESH = pl.DeviceIdType.MESH

D = 4096
BLK = 256
NB = 16
NS = 8
T = 64
RIDGE = 0.25
EPSILON = 1e-06
TURN = 1.0 / (2.0 * math.pi)
NORM = math.sqrt(2.0 / (16 * D))
SINE = (6.283164044251588, -41.337142364570006, 81.34076867837481, -70.99343135659183)
COEF = tuple(c * NORM for c in SINE)


def hadamard():
    i = lax.broadcasted_iota(jnp.int32, (BLK, BLK), 0)
    j = lax.broadcasted_iota(jnp.int32, (BLK, BLK), 1)
    v = i & j
    v = v ^ (v >> 4)
    v = v ^ (v >> 2)
    v = v ^ (v >> 1)
    return (1 - 2 * (v & 1)).astype(f32)


def butterfly(values):
    v = list(values)
    h = 1
    while h < len(v):
        for i in range(0, len(v), 2 * h):
            for k in range(i, i + h):
                v[k], v[k + h] = v[k] + v[k + h], v[k] - v[k + h]
        h *= 2
    return v


def split(x):
    hi = x.astype(bf16)
    return hi, (x - hi.astype(f32)).astype(bf16)


def dot(a, b):
    return jnp.dot(a, b, preferred_element_type=f32)


def dot_t(a, b):
    return lax.dot_general(a, b, (((1,), (1,)), ((), ())), preferred_element_type=f32)


def row_sums(x):
    ones = jnp.ones((8, x.shape[1]), f32)
    return lax.dot_general(
        ones, x, (((1,), (1,)), ((), ())), precision=lax.Precision.HIGHEST, preferred_element_type=f32
    )


def column(row):
    wide = jnp.concatenate([row, row], axis=1)
    return jnp.transpose(wide)[:T, 0:1]


def columns_of_parameters(gauss, scale, phase, col):
    for b in range(D // 128):
        at = slice(b * 128, (b + 1) * 128)
        block = jnp.concatenate(
            [
                gauss[:, at],
                scale[:, at] * (TURN / D),
                phase[:, at] * TURN,
                jnp.zeros((2, 128), f32),
            ],
            axis=0,
        )
        col[at, :] = jnp.transpose(block)


def spread_blocks(s, sign, emb, h, y):
    def body(a, _):
        o = pl.multiple_of(a * BLK, BLK)
        signs = (2 * sign[s : s + 1, pl.ds(o, BLK)] - 1).astype(f32)
        y[pl.ds(o, BLK), :] = dot((h * signs).astype(bf16), emb[pl.ds(o, BLK), :])
        return 0

    lax.fori_loop(0, NB, body, 0, unroll=4)


def spread_across(y, sp):
    def body(r, _):
        o = pl.multiple_of(r * 8, 8)
        for half in range(2):
            lanes = slice(half * 128, (half + 1) * 128)
            v = butterfly([y[pl.ds(a * BLK + o, 8), lanes] for a in range(NB)])
            for a in range(NB):
                sp[half, pl.ds(a * BLK + o, 8), :] = v[a]
        return 0

    lax.fori_loop(0, BLK // 8, body, 0)


def permute(perm, sp, y):
    groups = 8
    sub = lax.broadcasted_iota(jnp.int32, (8, 128), 0)

    def body(jb, _):
        o = pl.multiple_of(jb * 8 * groups, 8 * groups)
        for q in range(groups):
            at = pl.multiple_of(o + q * 8, 8)
            idx = [perm[o + q * 8 + k] for k in range(8)]
            for half in range(2):
                rows = [jnp.broadcast_to(sp[half, pl.ds(i, 1), :], (8, 128)) for i in idx]
                acc = rows[0]
                for k in range(1, 8):
                    acc = jnp.where(sub == k, rows[k], acc)
                y[pl.ds(at, 8), half * 128 : (half + 1) * 128] = acc
        return 0

    lax.fori_loop(0, D // (8 * groups), body, 0)


def mix_across(s, y, col, z):
    def body(r, _):
        o = pl.multiple_of(r * 16, 16)
        gauss = [jnp.broadcast_to(col[pl.ds(a * BLK + o, 16), s : s + 1], (16, 128)) for a in range(NB)]
        for half in range(2):
            lanes = slice(half * 128, (half + 1) * 128)
            v = butterfly([y[pl.ds(a * BLK + o, 16), lanes] * gauss[a] for a in range(NB)])
            for a in range(NB):
                hi, lo = split(v[a])
                z[a, pl.ds(o, 16), lanes] = hi
                z[a, pl.ds(BLK + o, 16), lanes] = lo
        return 0

    lax.fori_loop(0, BLK // 16, body, 0)


def cosine(turns):
    x = 0.25 - jnp.abs(turns - jnp.round(turns))
    u = x * x
    p = COEF[3]
    for c in COEF[2::-1]:
        p = p * u + c
    return p * x


def features(s, z, h2, col, fh, fl, also=None):
    def body(a, _):
        o = pl.multiple_of(a * BLK, BLK)
        scale = col[pl.ds(o, BLK), 2 + s : 3 + s]
        phase = col[pl.ds(o, BLK), 4 + s : 5 + s]
        hi, lo = split(cosine(dot(h2, z[a]) * scale + phase))
        fh[s, a] = hi
        fl[s, a] = lo
        if also is not None:
            also(a, hi, lo)
        return 0

    lax.fori_loop(0, NB, body, 0, unroll=2)


def kernel(
    emb_h, sign_h, perm_h, gauss_h, scale_h, phase_h, res_h, dire_h,
    applied_out, step_out, conj_out,
    emb, sign, gauss, scale, phase, res, dire, perm0, perm1, in_sem, out_sem,
    y, sp, z, fh, fl, col,
    da, db, stat, stat2, pacc, psib, pchip, px, sa, sb, ra1, rb1, sa2, sb2, ra2, rb2, app, wide, pp, pp2, nn, nn2,
    d1_send, d1_recv, d2_send, d2_recv, st_send, st_recv, st2_send, st2_recv,
    p1_send, p1_recv, p2_send, p2_recv, i1_send, i1_recv, i2_send, i2_recv,
    pp_send, pp_recv, pp2_send, pp2_recv, n1_send, n1_recv, n2_send, n2_recv,
):
    ex = lax.axis_index("ex")
    st = lax.axis_index("stk")
    ez, ey = ex // 4, ex % 4

    def ring(i, k):
        return (i + k) % 4

    def ex_dev(dz, dy):
        return (ring(ez, dz) * 4 + ring(ey, dy), st)

    def st_dev(k):
        return (ex, (st + k) % NS)

    sibling = (ex, st + 1 - 2 * (st % 2))

    def remote(dev, src, dst, send, recv):
        return pltpu.make_async_remote_copy(
            src_ref=src, dst_ref=dst, send_sem=send, recv_sem=recv, device_id=dev, device_id_type=MESH
        )

    def each(n, f, first=1):
        def body(k, _):
            f(k)
            return 0

        lax.fori_loop(first, n, body, 0)

    def ex_k(k):
        return ex_dev(k // 4, k % 4)

    inputs = [
        pltpu.make_async_copy(src, dst, in_sem.at[i])
        for i, (src, dst) in enumerate(
            [
                (dire_h, dire), (res_h, res), (sign_h, sign), (emb_h, emb), (gauss_h, gauss),
                (scale_h, scale), (phase_h, phase), (perm_h.at[0], perm0), (perm_h.at[1], perm1),
            ]
        )
    ]
    for c in inputs:
        c.start()
    barrier = pltpu.get_barrier_semaphore()
    each(NB, lambda k: pl.semaphore_signal(barrier, inc=1, device_id=ex_k(k), device_id_type=MESH))
    each(NS, lambda k: pl.semaphore_signal(barrier, inc=1, device_id=st_dev(k), device_id_type=MESH))

    h = hadamard()
    hb = h.astype(bf16)
    h2 = jnp.concatenate([hb, hb], axis=1)

    inputs[0].wait()
    inputs[1].wait()
    own_a, own_b = ex, ey * 4 + ez
    da[own_a] = dire[:, 0, :]
    db[own_b] = dire[:, 1, :]

    pl.semaphore_wait(barrier, NB - 1 + NS - 1)

    def d1_copy(a, k):
        if a:
            return remote(ex_dev(0, k), da.at[own_a], da.at[own_a], d1_send.at[0, k], d1_recv.at[0, k])
        return remote(ex_dev(k, 0), db.at[own_b], db.at[own_b], d1_send.at[1, k], d1_recv.at[1, k])

    def d2_copy(a, k):
        four_a, four_b = da.at[pl.ds(ez * 4, 4)], db.at[pl.ds(ey * 4, 4)]
        if a:
            return remote(ex_dev(k, 0), four_a, four_a, d2_send.at[0, k], d2_recv.at[0, k])
        return remote(ex_dev(0, k), four_b, four_b, d2_send.at[1, k], d2_recv.at[1, k])

    def both(f):
        def go(k):
            f(True, k)
            f(False, k)

        each(4, go)

    both(lambda a, k: d1_copy(a, k).start())

    def st_copy(k):
        return remote(ex_k(k), stat.at[0], stat.at[k], st_send.at[k], st_recv.at[k])

    r2 = row_sums(jnp.concatenate([jnp.square(res[:, s, :]) for s in range(2)], axis=1))
    d2 = row_sums(jnp.concatenate([jnp.square(dire[:, s, :]) for s in range(2)], axis=1))
    stat[0] = jnp.concatenate([r2, d2], axis=1)
    each(NB, lambda k: st_copy(k).start())

    inputs[2].wait()
    inputs[3].wait()
    spread_blocks(0, sign, emb, h, y)
    spread_across(y, sp)
    for i in (4, 5, 6, 7, 8):
        inputs[i].wait()
    columns_of_parameters(gauss, scale, phase, col)
    permute(perm0, sp, y)

    both(lambda a, k: d1_copy(a, k).wait_recv())
    both(lambda a, k: d2_copy(a, k).start())

    mix_across(0, y, col, z)
    features(0, z, h2, col, fh, fl)

    each(NB, lambda k: st_copy(k).wait())
    stat2[0] = jnp.sum(stat[...], axis=0)

    def st2_copy(k):
        return remote(st_dev(k), stat2.at[0], stat2.at[k], st2_send.at[k], st2_recv.at[k])

    each(NS, lambda k: st2_copy(k).start())

    spread_blocks(1, sign, emb, h, y)
    spread_across(y, sp)
    permute(perm1, sp, y)
    mix_across(1, y, col, z)

    each(NS, lambda k: st2_copy(k).wait())
    totals = jnp.sum(stat2[...], axis=0)
    norm_old, d_norm = totals[:, :T], totals[:, T:]
    both(lambda a, k: d2_copy(a, k).wait_recv())

    def project(a, hi1, lo1):
        hi, lo = split(da[a])
        both0 = dot(jnp.concatenate([hi, lo], axis=0), fh[0, a])
        both0_lo = dot(hi, fl[0, a])
        hi, lo = split(db[(a % 4) * 4 + a // 4])
        both1 = dot(jnp.concatenate([hi, lo], axis=0), hi1)
        pacc[...] += (both0[:T] + both1[:T]) + (both0[T:] + both1[T:] + both0_lo + dot(hi, lo1))

    pacc[...] = jnp.zeros_like(pacc)
    features(1, z, h2, col, fh, fl, project)

    def p1_copy():
        return remote(sibling, pacc, psib, p1_send, p1_recv)

    p1_copy().start()
    p1_copy().wait_recv()
    pchip[...] = pacc[...] + psib[...]

    def p2_copy(k):
        return remote(st_dev(2 * k), pchip, px.at[k], p2_send.at[k], p2_recv.at[k])

    each(4, lambda k: p2_copy(k).start())
    px[0] = pchip[...]
    each(4, lambda k: p2_copy(k).wait_recv())
    projected = (px[0] + px[1]) + (px[2] + px[3])
    p_hi, p_lo = split(projected)
    p_both = jnp.concatenate([p_hi, p_lo], axis=0)

    pp_row = row_sums(jnp.square(projected))
    pp[0] = jnp.concatenate([pp_row, pp_row], axis=1)

    def pp_copy(k):
        return remote(ex_dev(0, k), pp.at[0], pp.at[k], pp_send.at[k], pp_recv.at[k])

    def pp2_copy(k):
        return remote(ex_dev(k, 0), pp2.at[0], pp2.at[k], pp2_send.at[k], pp2_recv.at[k])

    each(4, lambda k: pp_copy(k).start())

    def image(s, e):
        big = dot_t(p_both, fh[s, e])
        return big[:T] + big[T:] + dot_t(p_hi, fl[s, e])

    def i1_copy(a, near, far):
        if a:
            return remote(
                ex_dev(0, near), sa.at[near, far], ra1.at[near, far], i1_send.at[0, near, far], i1_recv.at[0, near, far]
            )
        return remote(
            ex_dev(near, 0), sb.at[near, far], rb1.at[near, far], i1_send.at[1, near, far], i1_recv.at[1, near, far]
        )

    def image_out(i):
        far, near = (i // 4 + 1) % 4, (i + 1) % 4
        sa[near, far] = image(0, ring(ez, far) * 4 + ring(ey, near))
        sb[near, far] = image(1, ring(ez, near) * 4 + ring(ey, far))

        @pl.when(near > 0)
        def _():
            i1_copy(True, near, far).start()
            i1_copy(False, near, far).start()

    each(16, image_out, 0)

    each(4, lambda k: pp_copy(k).wait())
    pp2[0] = jnp.sum(pp[...], axis=0)
    each(4, lambda k: pp2_copy(k).start())

    def i2_copy(a, k):
        if a:
            return remote(ex_dev(k, 0), sa2.at[k], ra2.at[k], i2_send.at[0, k], i2_recv.at[0, k])
        return remote(ex_dev(0, k), sb2.at[k], rb2.at[k], i2_send.at[1, k], i2_recv.at[1, k])

    def forward(far):
        for a, src, got, out in ((True, sa, ra1, sa2), (False, sb, rb1, sb2)):
            each(4, lambda near: i1_copy(a, near, far).wait_recv())
            out[far] = (src[0, far] + got[1, far]) + (got[2, far] + got[3, far])

    def forward_out(far):
        forward(far)
        i2_copy(True, far).start()
        i2_copy(False, far).start()

    each(4, forward_out)

    each(4, lambda k: pp2_copy(k).wait())
    p_norm = jnp.sum(pp2[...], axis=0)[:, :T]
    step = column(norm_old / (RIDGE * d_norm + p_norm))
    wide[0] = jnp.broadcast_to(step, (T, 128))
    step_copy = pltpu.make_async_copy(wide.at[0], step_out, out_sem.at[0])
    step_copy.start()

    forward(0)
    both(lambda a, k: i2_copy(a, k).wait_recv())
    squares = []
    for s, own, got in ((0, sa2, ra2), (1, sb2, rb2)):
        applied = RIDGE * dire[:, s, :] + ((own[0] + got[1]) + (got[2] + got[3]))
        app[:, s, :] = applied
        squares.append(jnp.square(res[:, s, :] - step * applied))
    app_copy = pltpu.make_async_copy(app, applied_out, out_sem.at[1])
    app_copy.start()
    n_row = row_sums(jnp.concatenate(squares, axis=1))
    nn[0] = jnp.concatenate([n_row, n_row], axis=1)

    def n1_copy(k):
        return remote(ex_k(k), nn.at[0], nn.at[k], n1_send.at[k], n1_recv.at[k])

    each(NB, lambda k: n1_copy(k).start())
    each(NB, lambda k: n1_copy(k).wait())
    nn2[0] = jnp.sum(nn[...], axis=0)

    def n2_copy(k):
        return remote(st_dev(k), nn2.at[0], nn2.at[k], n2_send.at[k], n2_recv.at[k])

    each(NS, lambda k: n2_copy(k).start())
    both(lambda a, k: d1_copy(a, k).wait_send())
    both(lambda a, k: d2_copy(a, k).wait_send())
    p1_copy().wait_send()
    each(4, lambda k: p2_copy(k).wait_send())

    def i1_sent(i):
        near, far = i // 4 + 1, i % 4
        i1_copy(True, near, far).wait_send()
        i1_copy(False, near, far).wait_send()

    each(12, i1_sent, 0)
    both(lambda a, k: i2_copy(a, k).wait_send())
    step_copy.wait()
    app_copy.wait()
    each(NS, lambda k: n2_copy(k).wait())
    norm_new = jnp.sum(nn2[...], axis=0)[:, :T]
    wide[1] = jnp.broadcast_to(column(norm_new / (norm_old + EPSILON)), (T, 128))
    conj_copy = pltpu.make_async_copy(wide.at[1], conj_out, out_sem.at[2])
    conj_copy.start()
    conj_copy.wait()


def local(embeddings, sign_bits, permutation, gaussian, scaling, phases, solution, residual, direction):
    hbm = pl.BlockSpec(memory_space=pltpu.HBM)
    dma = pltpu.SemaphoreType.DMA
    vmem = pltpu.VMEM
    block, tile = (T, BLK), (8, 128)
    applied, step, conjugacy = pl.pallas_call(
        kernel,
        out_shape=[
            jax.ShapeDtypeStruct(direction.shape, f32),
            jax.ShapeDtypeStruct((T, 128), f32),
            jax.ShapeDtypeStruct((T, 128), f32),
        ],
        in_specs=[hbm] * 8,
        out_specs=[hbm] * 3,
        scratch_shapes=[
            vmem((D, BLK), bf16),
            vmem((2, D), jnp.int32),
            vmem((2, D), f32),
            vmem((2, D), f32),
            vmem((2, D), f32),
            vmem(direction.shape, f32),
            vmem(direction.shape, f32),
            pltpu.SMEM((D,), jnp.int32),
            pltpu.SMEM((D,), jnp.int32),
            dma((9,)),
            dma((3,)),
            vmem((D, BLK), f32),
            vmem((2, D, 128), f32),
            vmem((NB, 2 * BLK, BLK), bf16),
            vmem((2, NB, BLK, BLK), bf16),
            vmem((2, NB, BLK, BLK), bf16),
            vmem((D, 8), f32),
            vmem((NB,) + block, f32),
            vmem((NB,) + block, f32),
            vmem((NB,) + tile, f32),
            vmem((NS,) + tile, f32),
            vmem(block, f32),
            vmem(block, f32),
            vmem(block, f32),
            vmem((4,) + block, f32),
            vmem((4, 4) + block, f32),
            vmem((4, 4) + block, f32),
            vmem((4, 4) + block, f32),
            vmem((4, 4) + block, f32),
            vmem((4,) + block, f32),
            vmem((4,) + block, f32),
            vmem((4,) + block, f32),
            vmem((4,) + block, f32),
            vmem(direction.shape, f32),
            vmem((2, T, 128), f32),
            vmem((4,) + tile, f32),
            vmem((4,) + tile, f32),
            vmem((NB,) + tile, f32),
            vmem((NS,) + tile, f32),
            dma((2, 4)), dma((2, 4)), dma((2, 4)), dma((2, 4)),
            dma((NB,)), dma((NB,)), dma((NS,)), dma((NS,)),
            dma, dma, dma((4,)), dma((4,)),
            dma((2, 4, 4)), dma((2, 4, 4)), dma((2, 4)), dma((2, 4)),
            dma((4,)), dma((4,)), dma((4,)), dma((4,)),
            dma((NB,)), dma((NB,)), dma((NS,)), dma((NS,)),
        ],
        compiler_params=pltpu.CompilerParams(
            collective_id=0, has_side_effects=True, vmem_limit_bytes=60 * 2**20
        ),
    )(embeddings, sign_bits, permutation, gaussian, scaling, phases, residual, direction)
    step = step[:, :1, None]
    conjugacy = conjugacy[:, :1, None]
    residual_next = residual - step * applied
    return solution + step * direction, residual_next, residual_next + conjugacy * direction


def solution(mesh):
    rows, stacks, blocks = P(None, "ex"), P("stk", None), P(None, "stk", "ex")
    return jax.shard_map(
        local,
        mesh=mesh,
        in_specs=(rows, stacks, stacks, stacks, stacks, stacks, blocks, blocks, blocks),
        out_specs=(blocks, blocks, blocks),
        check_vma=False,
    )
```

```python
import functools
import math

import jax
import jax.numpy as jnp
from jax import lax
from jax.experimental import pallas as pl
from jax.experimental.pallas import tpu as pltpu
from jax.sharding import PartitionSpec as P

f32, bf16 = jnp.float32, jnp.bfloat16
MESH = pl.DeviceIdType.MESH

D = 4096
BLK = 256
NB = 16
NS = 8
T = 64
RIDGE = 0.25
EPSILON = 1e-06
TURN = 1.0 / (2.0 * math.pi)
NORM = math.sqrt(2.0 / (16 * D))
SINE = (6.283164044251588, -41.337142364570006, 81.34076867837481, -70.99343135659183)
COEF = tuple(c * NORM for c in SINE)


def hadamard():
    i = lax.broadcasted_iota(jnp.int32, (BLK, BLK), 0)
    j = lax.broadcasted_iota(jnp.int32, (BLK, BLK), 1)
    v = i & j
    v = v ^ (v >> 4)
    v = v ^ (v >> 2)
    v = v ^ (v >> 1)
    return (1 - 2 * (v & 1)).astype(f32)


def butterfly(values):
    v = list(values)
    h = 1
    while h < len(v):
        for i in range(0, len(v), 2 * h):
            for k in range(i, i + h):
                v[k], v[k + h] = v[k] + v[k + h], v[k] - v[k + h]
        h *= 2
    return v


def split(x):
    hi = x.astype(bf16)
    return hi, (x - hi.astype(f32)).astype(bf16)


def dot(a, b):
    return jnp.dot(a, b, preferred_element_type=f32)


def dot_t(a, b):
    return lax.dot_general(a, b, (((1,), (1,)), ((), ())), preferred_element_type=f32)


def row_sums(x):
    ones = jnp.ones((8, x.shape[1]), f32)
    return lax.dot_general(
        ones, x, (((1,), (1,)), ((), ())), precision=lax.Precision.HIGHEST, preferred_element_type=f32
    )


def column(row):
    wide = jnp.concatenate([row, row], axis=1)
    return jnp.transpose(wide)[:T, 0:1]


def columns_of_parameters(gauss, scale, phase, col):
    for b in range(D // 128):
        at = slice(b * 128, (b + 1) * 128)
        block = jnp.concatenate(
            [
                gauss[:, at],
                scale[:, at] * (TURN / D),
                phase[:, at] * TURN,
                jnp.zeros((2, 128), f32),
            ],
            axis=0,
        )
        col[at, :] = jnp.transpose(block)


def spread_block(s, a, sign, emb, h, y):
    o = pl.multiple_of(a * BLK, BLK)
    signs = (2 * sign[s : s + 1, pl.ds(o, BLK)] - 1).astype(f32)
    y[pl.ds(o, BLK), :] = dot((h * signs).astype(bf16), emb[pl.ds(o, BLK), :])


def spread_across(r, y, sp):
    o = pl.multiple_of(r * 8, 8)
    for half in range(2):
        lanes = slice(half * 128, (half + 1) * 128)
        v = butterfly([y[pl.ds(a * BLK + o, 8), lanes] for a in range(NB)])
        for a in range(NB):
            sp[half, pl.ds(a * BLK + o, 8), :] = v[a]


def permute(base, rows, perm, sp, y, sub):
    for q in range(rows // 8):
        at = pl.multiple_of(base + q * 8, 8)
        idx = [perm[base + q * 8 + k] for k in range(8)]
        for half in range(2):
            lanes = slice(half * 128, (half + 1) * 128)
            if sub is None:
                out = y.at[pl.ds(at, 8), lanes]
                for k in range(8):
                    out[k : k + 1, :] = sp[half, pl.ds(idx[k], 1), :]
            else:
                row = [jnp.broadcast_to(sp[half, pl.ds(i, 1), :], (8, 128)) for i in idx]
                acc = row[0]
                for k in range(1, 8):
                    acc = jnp.where(sub == k, row[k], acc)
                y[pl.ds(at, 8), lanes] = acc


def mix_across(r, y, bc, z):
    o = pl.multiple_of(r * 16, 16)
    for half in range(2):
        lanes = slice(half * 128, (half + 1) * 128)
        v = butterfly(
            [
                y[pl.ds(a * BLK + o, 16), lanes]
                * bc[0, pl.ds(a * BLK + o, 16), :]
                for a in range(NB)
            ]
        )
        for a in range(NB):
            hi, lo = split(v[a])
            z[a, pl.ds(o, 16), lanes] = hi
            z[a, pl.ds(BLK + o, 16), lanes] = lo


def loop(n, f, unroll=1):
    def body(i, _):
        f(i)
        return 0

    lax.fori_loop(0, n, body, 0, unroll=unroll)


def cosine(turns):
    x = 0.25 - jnp.abs(turns - jnp.round(turns))
    u = x * x
    p = COEF[3]
    for c in COEF[2::-1]:
        p = p * u + c
    return p * x


def spread_parameters(s, a, col, bc):
    at = pl.ds(pl.multiple_of(a * BLK, BLK), BLK)
    for v in range(3):
        bc[v, at, :] = jnp.broadcast_to(col[at, 2 * v + s : 2 * v + s + 1], (BLK, 128))


def features(s, a, ang, bc, fh, fl, also=None):
    o = pl.multiple_of(a * BLK, BLK)
    for c in range(8):
        rows = slice(c * 32, (c + 1) * 32)
        at = pl.ds(o + c * 32, 32)
        for half in range(2):
            lanes = slice(half * 128, (half + 1) * 128)
            hi, lo = split(cosine(ang[rows, lanes] * bc[1, at, :] + bc[2, at, :]))
            fh[s, a, rows, lanes] = hi
            fl[s, a, rows, lanes] = lo
        if also is not None:
            also(c)


def kernel(
    emb_h, sign_h, perm_h, gauss_h, scale_h, phase_h, res_h, dire_h,
    applied_out, step_out, conj_out,
    emb, sign, gauss, scale, phase, res, dire, perm0, perm1, in_sem, out_sem,
    y, sp, y1, sp1, z, fh, fl, col, bc0, bc1, ang0, ang1,
    da, db, stat, stat2, pacc, psib, pchip, px, sa, sb, ra1, rb1, sa2, sb2, ra2, rb2, app, wide, pp, pp2, nn, nn2,
    d1_send, d1_recv, d2_send, d2_recv, st_send, st_recv, st2_send, st2_recv,
    p1_send, p1_recv, p2_send, p2_recv, i1_send, i1_recv, i2_send, i2_recv,
    pp_send, pp_recv, pp2_send, pp2_recv, n1_send, n1_recv, n2_send, n2_recv,
):
    ex = lax.axis_index("ex")
    st = lax.axis_index("stk")
    ez, ey = ex // 4, ex % 4

    def ring(i, k):
        return (i + k) % 4

    def ex_dev(dz, dy):
        return (ring(ez, dz) * 4 + ring(ey, dy), st)

    def st_dev(k):
        return (ex, (st + k) % NS)

    sibling = (ex, st + 1 - 2 * (st % 2))

    def remote(dev, src, dst, send, recv):
        return pltpu.make_async_remote_copy(
            src_ref=src, dst_ref=dst, send_sem=send, recv_sem=recv, device_id=dev, device_id_type=MESH
        )

    def each(n, f, first=1):
        def body(k, _):
            f(k)
            return 0

        lax.fori_loop(first, n, body, 0)

    def ex_k(k):
        return ex_dev(k // 4, k % 4)

    inputs = [
        pltpu.make_async_copy(src, dst, in_sem.at[i])
        for i, (src, dst) in enumerate(
            [
                (dire_h, dire), (res_h, res), (sign_h, sign), (emb_h, emb), (gauss_h, gauss),
                (scale_h, scale), (phase_h, phase), (perm_h.at[0], perm0), (perm_h.at[1], perm1),
            ]
        )
    ]
    for c in inputs:
        c.start()
    barrier = pltpu.get_barrier_semaphore()
    each(NB, lambda k: pl.semaphore_signal(barrier, inc=1, device_id=ex_k(k), device_id_type=MESH))
    each(NS, lambda k: pl.semaphore_signal(barrier, inc=1, device_id=st_dev(k), device_id_type=MESH))

    h = hadamard()
    hb = h.astype(bf16)
    h2 = jnp.concatenate([hb, hb], axis=1)

    inputs[0].wait()
    inputs[1].wait()
    own_a, own_b = ex, ey * 4 + ez
    da[own_a] = dire[:, 0, :]
    db[own_b] = dire[:, 1, :]

    inputs[2].wait()
    inputs[3].wait()
    loop(NB, lambda a: spread_block(0, a, sign, emb, h, y), 4)
    loop(32, lambda r: spread_across(r, y, sp), 2)
    pl.semaphore_wait(barrier, NB - 1 + NS - 1)

    def d1_copy(a, k):
        if a:
            return remote(ex_dev(0, k), da.at[own_a], da.at[own_a], d1_send.at[0, k], d1_recv.at[0, k])
        return remote(ex_dev(k, 0), db.at[own_b], db.at[own_b], d1_send.at[1, k], d1_recv.at[1, k])

    def d2_copy(a, k):
        four_a, four_b = da.at[pl.ds(ez * 4, 4)], db.at[pl.ds(ey * 4, 4)]
        if a:
            return remote(ex_dev(k, 0), four_a, four_a, d2_send.at[0, k], d2_recv.at[0, k])
        return remote(ex_dev(0, k), four_b, four_b, d2_send.at[1, k], d2_recv.at[1, k])

    def both(f):
        def go(k):
            f(True, k)
            f(False, k)

        each(4, go)

    both(lambda a, k: d1_copy(a, k).start())

    def st_copy(k):
        return remote(ex_k(k), stat.at[0], stat.at[k], st_send.at[k], st_recv.at[k])

    r2 = row_sums(jnp.concatenate([jnp.square(res[:, s, :]) for s in range(2)], axis=1))
    d2 = row_sums(jnp.concatenate([jnp.square(dire[:, s, :]) for s in range(2)], axis=1))
    stat[0] = jnp.concatenate([r2, d2], axis=1)
    each(NB, lambda k: st_copy(k).start())

    for i in (4, 5, 6, 7, 8):
        inputs[i].wait()
    columns_of_parameters(gauss, scale, phase, col)
    sub = lax.broadcasted_iota(jnp.int32, (8, 128), 0)

    def permute_spread(i):
        for q in range(2):
            spread_block(1, 2 * i + q, sign, emb, h, y1)
            spread_parameters(0, 2 * i + q, col, bc0)
            permute(pl.multiple_of(i * 256 + q * 128, 128), 128, perm0, sp, y, sub)

    def permute_spread_across(i):
        for q in range(4):
            spread_across(4 * i + q, y1, sp1)
            if q < 2:
                spread_parameters(1, 2 * i + q, col, bc1)
            permute(pl.multiple_of(D // 2 + i * 256 + q * 64, 64), 64, perm0, sp, y, sub)

    loop(8, permute_spread)
    loop(8, permute_spread_across)

    both(lambda a, k: d1_copy(a, k).wait_recv())
    both(lambda a, k: d2_copy(a, k).start())

    def mix_permute(i):
        mix_across(i, y, bc0, z)
        permute(pl.multiple_of(i * 64, 64), 64, perm1, sp1, y1, None)

    def features_permute(j):
        for q in range(2):
            i = 2 * j + q

            def part(c):
                n = (256 - 64) // 8
                permute(pl.multiple_of(16 * 64 + i * (256 - 64) + c * n, 8), n, perm1, sp1, y1, None)

            features(0, i, (ang0, ang1)[q], bc0, fh, fl, part)
            (ang1, ang0)[q][...] = dot(h2, z[(i + 1) % NB])

    loop(NB, mix_permute)
    ang0[...] = dot(h2, z[0])
    loop(NB // 2, features_permute)

    each(NB, lambda k: st_copy(k).wait())
    stat2[0] = jnp.sum(stat[...], axis=0)

    def st2_copy(k):
        return remote(st_dev(k), stat2.at[0], stat2.at[k], st2_send.at[k], st2_recv.at[k])

    each(NS, lambda k: st2_copy(k).start())

    loop(NB, lambda i: mix_across(i, y1, bc1, z))

    each(NS, lambda k: st2_copy(k).wait())
    totals = jnp.sum(stat2[...], axis=0)
    norm_old, d_norm = totals[:, :T], totals[:, T:]
    both(lambda a, k: d2_copy(a, k).wait_recv())

    def project(a):
        part = 0.0
        for s, block in ((0, da[a]), (1, db[(a % 4) * 4 + a // 4])):
            hi, lo = split(block)
            big = dot(jnp.concatenate([hi, lo], axis=0), fh[s, a])
            part += big[:T] + (big[T:] + dot(hi, fl[s, a]))
        pacc[...] += part

    def features_project(j):
        for q in range(2):
            i = 2 * j + q
            features(1, i, (ang0, ang1)[q], bc1, fh, fl)
            (ang1, ang0)[q][...] = dot(h2, z[(i + 1) % NB])
            project(i)

    pacc[...] = jnp.zeros_like(pacc)
    ang0[...] = dot(h2, z[0])
    loop(NB // 2, features_project)

    def p1_copy():
        return remote(sibling, pacc, psib, p1_send, p1_recv)

    p1_copy().start()
    p1_copy().wait_recv()
    pchip[...] = pacc[...] + psib[...]

    def p2_copy(k):
        return remote(st_dev(2 * k), pchip, px.at[k], p2_send.at[k], p2_recv.at[k])

    each(4, lambda k: p2_copy(k).start())
    px[0] = pchip[...]
    each(4, lambda k: p2_copy(k).wait_recv())
    projected = (px[0] + px[1]) + (px[2] + px[3])
    p_hi, p_lo = split(projected)
    p_both = jnp.concatenate([p_hi, p_lo], axis=0)

    pp_row = row_sums(jnp.square(projected))
    pp[0] = jnp.concatenate([pp_row, pp_row], axis=1)

    def pp_copy(k):
        return remote(ex_dev(0, k), pp.at[0], pp.at[k], pp_send.at[k], pp_recv.at[k])

    def pp2_copy(k):
        return remote(ex_dev(k, 0), pp2.at[0], pp2.at[k], pp2_send.at[k], pp2_recv.at[k])

    each(4, lambda k: pp_copy(k).start())

    def image(s, e):
        big = dot_t(p_both, fh[s, e])
        return big[:T] + big[T:] + dot_t(p_hi, fl[s, e])

    def i1_copy(a, near, far):
        if a:
            return remote(
                ex_dev(0, near), sa.at[near, far], ra1.at[near, far], i1_send.at[0, near, far], i1_recv.at[0, near, far]
            )
        return remote(
            ex_dev(near, 0), sb.at[near, far], rb1.at[near, far], i1_send.at[1, near, far], i1_recv.at[1, near, far]
        )

    def image_out(i):
        far, near = (i // 4 + 1) % 4, (i + 1) % 4
        sa[near, far] = image(0, ring(ez, far) * 4 + ring(ey, near))
        sb[near, far] = image(1, ring(ez, near) * 4 + ring(ey, far))

        @pl.when(near > 0)
        def _():
            i1_copy(True, near, far).start()
            i1_copy(False, near, far).start()

    each(16, image_out, 0)

    each(4, lambda k: pp_copy(k).wait())
    pp2[0] = jnp.sum(pp[...], axis=0)
    each(4, lambda k: pp2_copy(k).start())

    def i2_copy(a, k):
        if a:
            return remote(ex_dev(k, 0), sa2.at[k], ra2.at[k], i2_send.at[0, k], i2_recv.at[0, k])
        return remote(ex_dev(0, k), sb2.at[k], rb2.at[k], i2_send.at[1, k], i2_recv.at[1, k])

    def forward(far):
        for a, src, got, out in ((True, sa, ra1, sa2), (False, sb, rb1, sb2)):
            each(4, lambda near: i1_copy(a, near, far).wait_recv())
            out[far] = (src[0, far] + got[1, far]) + (got[2, far] + got[3, far])

    def forward_out(far):
        forward(far)
        i2_copy(True, far).start()
        i2_copy(False, far).start()

    each(4, forward_out)

    each(4, lambda k: pp2_copy(k).wait())
    p_norm = jnp.sum(pp2[...], axis=0)[:, :T]
    step = column(norm_old / (RIDGE * d_norm + p_norm))
    wide[0] = jnp.broadcast_to(step, (T, 128))
    step_copy = pltpu.make_async_copy(wide.at[0], step_out, out_sem.at[0])
    step_copy.start()

    forward(0)
    both(lambda a, k: i2_copy(a, k).wait_recv())
    squares = []
    for s, own, got in ((0, sa2, ra2), (1, sb2, rb2)):
        applied = RIDGE * dire[:, s, :] + ((own[0] + got[1]) + (got[2] + got[3]))
        app[:, s, :] = applied
        squares.append(jnp.square(res[:, s, :] - step * applied))
    app_copy = pltpu.make_async_copy(app, applied_out, out_sem.at[1])
    app_copy.start()
    n_row = row_sums(jnp.concatenate(squares, axis=1))
    nn[0] = jnp.concatenate([n_row, n_row], axis=1)

    def n1_copy(k):
        return remote(ex_k(k), nn.at[0], nn.at[k], n1_send.at[k], n1_recv.at[k])

    each(NB, lambda k: n1_copy(k).start())
    each(NB, lambda k: n1_copy(k).wait())
    nn2[0] = jnp.sum(nn[...], axis=0)

    def n2_copy(k):
        return remote(st_dev(k), nn2.at[0], nn2.at[k], n2_send.at[k], n2_recv.at[k])

    each(NS, lambda k: n2_copy(k).start())
    both(lambda a, k: d1_copy(a, k).wait_send())
    both(lambda a, k: d2_copy(a, k).wait_send())
    p1_copy().wait_send()
    each(4, lambda k: p2_copy(k).wait_send())

    def i1_sent(i):
        near, far = i // 4 + 1, i % 4
        i1_copy(True, near, far).wait_send()
        i1_copy(False, near, far).wait_send()

    each(12, i1_sent, 0)
    both(lambda a, k: i2_copy(a, k).wait_send())
    step_copy.wait()
    app_copy.wait()
    each(NS, lambda k: n2_copy(k).wait())
    norm_new = jnp.sum(nn2[...], axis=0)[:, :T]
    wide[1] = jnp.broadcast_to(column(norm_new / (norm_old + EPSILON)), (T, 128))
    conj_copy = pltpu.make_async_copy(wide.at[1], conj_out, out_sem.at[2])
    conj_copy.start()
    conj_copy.wait()


def local(embeddings, sign_bits, permutation, gaussian, scaling, phases, solution, residual, direction):
    hbm = pl.BlockSpec(memory_space=pltpu.HBM)
    dma = pltpu.SemaphoreType.DMA
    vmem = pltpu.VMEM
    block, tile = (T, BLK), (8, 128)
    applied, step, conjugacy = pl.pallas_call(
        kernel,
        out_shape=[
            jax.ShapeDtypeStruct(direction.shape, f32),
            jax.ShapeDtypeStruct((T, 128), f32),
            jax.ShapeDtypeStruct((T, 128), f32),
        ],
        in_specs=[hbm] * 8,
        out_specs=[hbm] * 3,
        scratch_shapes=[
            vmem((D, BLK), bf16),
            vmem((2, D), jnp.int32),
            vmem((2, D), f32),
            vmem((2, D), f32),
            vmem((2, D), f32),
            vmem(direction.shape, f32),
            vmem(direction.shape, f32),
            pltpu.SMEM((D,), jnp.int32),
            pltpu.SMEM((D,), jnp.int32),
            dma((9,)),
            dma((3,)),
            vmem((D, BLK), f32),
            vmem((2, D, 128), f32),
            vmem((D, BLK), f32),
            vmem((2, D, 128), f32),
            vmem((NB, 2 * BLK, BLK), bf16),
            vmem((2, NB, BLK, BLK), bf16),
            vmem((2, NB, BLK, BLK), bf16),
            vmem((D, 8), f32),
            vmem((3, D, 128), f32),
            vmem((3, D, 128), f32),
            vmem((BLK, BLK), f32),
            vmem((BLK, BLK), f32),
            vmem((NB,) + block, f32),
            vmem((NB,) + block, f32),
            vmem((NB,) + tile, f32),
            vmem((NS,) + tile, f32),
            vmem(block, f32),
            vmem(block, f32),
            vmem(block, f32),
            vmem((4,) + block, f32),
            vmem((4, 4) + block, f32),
            vmem((4, 4) + block, f32),
            vmem((4, 4) + block, f32),
            vmem((4, 4) + block, f32),
            vmem((4,) + block, f32),
            vmem((4,) + block, f32),
            vmem((4,) + block, f32),
            vmem((4,) + block, f32),
            vmem(direction.shape, f32),
            vmem((2, T, 128), f32),
            vmem((4,) + tile, f32),
            vmem((4,) + tile, f32),
            vmem((NB,) + tile, f32),
            vmem((NS,) + tile, f32),
            dma((2, 4)), dma((2, 4)), dma((2, 4)), dma((2, 4)),
            dma((NB,)), dma((NB,)), dma((NS,)), dma((NS,)),
            dma, dma, dma((4,)), dma((4,)),
            dma((2, 4, 4)), dma((2, 4, 4)), dma((2, 4)), dma((2, 4)),
            dma((4,)), dma((4,)), dma((4,)), dma((4,)),
            dma((NB,)), dma((NB,)), dma((NS,)), dma((NS,)),
        ],
        compiler_params=pltpu.CompilerParams(
            collective_id=0, has_side_effects=True, vmem_limit_bytes=60 * 2**20
        ),
    )(embeddings, sign_bits, permutation, gaussian, scaling, phases, residual, direction)
    step = step[:, :1, None]
    conjugacy = conjugacy[:, :1, None]
    residual_next = residual - step * applied
    return solution + step * direction, residual_next, residual_next + conjugacy * direction


def solution(mesh):
    rows, stacks, blocks = P(None, "ex"), P("stk", None), P(None, "stk", "ex")
    return jax.shard_map(
        local,
        mesh=mesh,
        in_specs=(rows, stacks, stacks, stacks, stacks, stacks, blocks, blocks, blocks),
        out_specs=(blocks, blocks, blocks),
        check_vma=False,
    )
```

```python
import functools
import math

import jax
import jax.numpy as jnp
from jax import lax
from jax.experimental import pallas as pl
from jax.experimental.pallas import tpu as pltpu
from jax.sharding import PartitionSpec as P

f32, bf16 = jnp.float32, jnp.bfloat16
MESH = pl.DeviceIdType.MESH

D = 4096
BLK = 256
NB = 16
NS = 8
T = 64
RIDGE = 0.25
EPSILON = 1e-06
TURN = 1.0 / (2.0 * math.pi)
NORM = math.sqrt(2.0 / (16 * D))
SINE = (6.283164044251588, -41.337142364570006, 81.34076867837481, -70.99343135659183)
COEF = tuple(c * NORM for c in SINE)


def hadamard():
    i = lax.broadcasted_iota(jnp.int32, (BLK, BLK), 0)
    j = lax.broadcasted_iota(jnp.int32, (BLK, BLK), 1)
    v = i & j
    v = v ^ (v >> 4)
    v = v ^ (v >> 2)
    v = v ^ (v >> 1)
    return (1 - 2 * (v & 1)).astype(f32)


def butterfly(values):
    v = list(values)
    h = 1
    while h < len(v):
        for i in range(0, len(v), 2 * h):
            for k in range(i, i + h):
                v[k], v[k + h] = v[k] + v[k + h], v[k] - v[k + h]
        h *= 2
    return v


def split(x):
    hi = x.astype(bf16)
    return hi, (x - hi.astype(f32)).astype(bf16)


def dot(a, b):
    return jnp.dot(a, b, preferred_element_type=f32)


def dot_t(a, b):
    return lax.dot_general(a, b, (((1,), (1,)), ((), ())), preferred_element_type=f32)


def row_sums(x):
    ones = jnp.ones((8, x.shape[1]), f32)
    return lax.dot_general(
        ones, x, (((1,), (1,)), ((), ())), precision=lax.Precision.HIGHEST, preferred_element_type=f32
    )


def column(row):
    wide = jnp.concatenate([row, row], axis=1)
    return jnp.transpose(wide)[:T, 0:1]


def columns_of_parameters(gauss, scale, phase, col):
    for b in range(D // 128):
        at = slice(b * 128, (b + 1) * 128)
        block = jnp.concatenate(
            [
                gauss[:, at],
                scale[:, at] * (TURN / D),
                phase[:, at] * TURN,
                jnp.zeros((2, 128), f32),
            ],
            axis=0,
        )
        col[at, :] = jnp.transpose(block)


def spread_block(s, a, sign, emb, h, y):
    o = pl.multiple_of(a * BLK, BLK)
    signs = (2 * sign[s : s + 1, pl.ds(o, BLK)] - 1).astype(f32)
    y[pl.ds(o, BLK), :] = dot((h * signs).astype(bf16), emb[pl.ds(o, BLK), :])


def spread_across(r, y, sp):
    o = pl.multiple_of(r * 8, 8)
    for half in range(2):
        lanes = slice(half * 128, (half + 1) * 128)
        v = butterfly([y[pl.ds(a * BLK + o, 8), lanes] for a in range(NB)])
        for a in range(NB):
            sp[pl.ds(2 * (a * BLK + o) + half, 8, stride=2), :] = v[a]


def permute(base, rows, perm, sp, yg):
    out = yg.at[pl.ds(pl.multiple_of(2 * base, 2 * 8), 2 * rows)]
    for k in range(rows):
        out[2 * k : 2 * k + 2, :] = sp[pl.ds(perm[base + k], 2), :]


def mix_across(r, yg, bc, z):
    o = pl.multiple_of(r * 16, 16)
    for half in range(2):
        lanes = slice(half * 128, (half + 1) * 128)
        v = butterfly(
            [
                yg[pl.ds(2 * (a * BLK + o) + half, 16, stride=2), :] * bc[0, pl.ds(a * BLK + o, 16), :]
                for a in range(NB)
            ]
        )
        for a in range(NB):
            hi, lo = split(v[a])
            z[a, pl.ds(o, 16), lanes] = hi
            z[a, pl.ds(BLK + o, 16), lanes] = lo


def loop(n, f, unroll=1):
    def body(i, _):
        f(i)
        return 0

    lax.fori_loop(0, n, body, 0, unroll=unroll)


def cosine(turns):
    x = 0.25 - jnp.abs(turns - jnp.round(turns))
    u = x * x
    p = COEF[3]
    for c in COEF[2::-1]:
        p = p * u + c
    return p * x


def spread_parameters(s, a, col, bc):
    at = pl.ds(pl.multiple_of(a * BLK, BLK), BLK)
    for v in range(3):
        bc[v, at, :] = jnp.broadcast_to(col[at, 2 * v + s : 2 * v + s + 1], (BLK, 128))


def features(s, a, ang, bc, fh, fl, also=None):
    o = pl.multiple_of(a * BLK, BLK)
    for c in range(8):
        rows = slice(c * 32, (c + 1) * 32)
        at = pl.ds(o + c * 32, 32)
        for half in range(2):
            lanes = slice(half * 128, (half + 1) * 128)
            hi, lo = split(cosine(ang[rows, lanes] * bc[1, at, :] + bc[2, at, :]))
            fh[s, a, rows, lanes] = hi
            fl[s, a, rows, lanes] = lo
        if also is not None:
            also(c)


def kernel(
    emb_h, sign_h, perm_h, gauss_h, scale_h, phase_h, res_h, dire_h,
    applied_out, step_out, conj_out,
    emb, sign, gauss, scale, phase, res, dire, pv, pv2, perm0, perm1, in_sem, perm_sem, out_sem,
    y, sp, yg, sp1, yg1, z, fh, fl, col, bc0, bc1, ang0, ang1,
    da, db, pacc, psib, pchip, px, sa, sb, ra1, rb1, sa2, sb2, ra2, rb2, app, wide, pp, pp2, nn, nn2,
    d1_send, d1_recv, d2_send, d2_recv,
    p1_send, p1_recv, p2_send, p2_recv, i1_send, i1_recv, i2_send, i2_recv,
    pp_send, pp_recv, pp2_send, pp2_recv, n1_send, n1_recv, n2_send, n2_recv,
):
    ex = lax.axis_index("ex")
    st = lax.axis_index("stk")
    ez, ey = ex // 4, ex % 4

    def ring(i, k):
        return (i + k) % 4

    def ex_dev(dz, dy):
        return (ring(ez, dz) * 4 + ring(ey, dy), st)

    def st_dev(k):
        return (ex, (st + k) % NS)

    sibling = (ex, st + 1 - 2 * (st % 2))

    def remote(dev, src, dst, send, recv):
        return pltpu.make_async_remote_copy(
            src_ref=src, dst_ref=dst, send_sem=send, recv_sem=recv, device_id=dev, device_id_type=MESH
        )

    def each(n, f, first=1):
        def body(k, _):
            f(k)
            return 0

        lax.fori_loop(first, n, body, 0)

    def ex_k(k):
        return ex_dev(k // 4, k % 4)

    inputs = [
        pltpu.make_async_copy(src, dst, in_sem.at[i])
        for i, (src, dst) in enumerate(
            [
                (dire_h, dire), (res_h, res), (sign_h, sign), (emb_h, emb), (gauss_h, gauss),
                (scale_h, scale), (phase_h, phase), (perm_h, pv),
            ]
        )
    ]
    for c in inputs:
        c.start()
    barrier = pltpu.get_barrier_semaphore()
    each(NB, lambda k: pl.semaphore_signal(barrier, inc=1, device_id=ex_k(k), device_id_type=MESH))
    each(NS, lambda k: pl.semaphore_signal(barrier, inc=1, device_id=st_dev(k), device_id_type=MESH))

    h = hadamard()
    hb = h.astype(bf16)
    h2 = jnp.concatenate([hb, hb], axis=1)

    inputs[0].wait()
    inputs[1].wait()
    own_a, own_b = ex, ey * 4 + ez
    da[own_a] = dire[:, 0, :]
    db[own_b] = dire[:, 1, :]

    inputs[7].wait()
    pv2[...] = 2 * pv[...]
    perm_copies = [
        pltpu.make_async_copy(pv2.at[s], p, perm_sem.at[s]) for s, p in enumerate((perm0, perm1))
    ]
    for c in perm_copies:
        c.start()
    inputs[2].wait()
    inputs[3].wait()
    loop(NB, lambda a: spread_block(0, a, sign, emb, h, y), 4)
    loop(32, lambda r: spread_across(r, y, sp), 2)
    pl.semaphore_wait(barrier, NB - 1 + NS - 1)

    def d1_copy(a, k):
        if a:
            return remote(ex_dev(0, k), da.at[own_a], da.at[own_a], d1_send.at[0, k], d1_recv.at[0, k])
        return remote(ex_dev(k, 0), db.at[own_b], db.at[own_b], d1_send.at[1, k], d1_recv.at[1, k])

    def d2_copy(a, k):
        four_a, four_b = da.at[pl.ds(ez * 4, 4)], db.at[pl.ds(ey * 4, 4)]
        if a:
            return remote(ex_dev(k, 0), four_a, four_a, d2_send.at[0, k], d2_recv.at[0, k])
        return remote(ex_dev(0, k), four_b, four_b, d2_send.at[1, k], d2_recv.at[1, k])

    def both(f):
        def go(k):
            f(True, k)
            f(False, k)

        each(4, go)

    both(lambda a, k: d1_copy(a, k).start())

    r2 = row_sums(jnp.concatenate([jnp.square(res[:, s, :]) for s in range(2)], axis=1))
    d2 = row_sums(jnp.concatenate([jnp.square(dire[:, s, :]) for s in range(2)], axis=1))
    pacc[...] = jnp.zeros_like(pacc)
    pacc[T:, :128] = jnp.concatenate([r2, d2], axis=1)

    for i in (4, 5, 6):
        inputs[i].wait()
    for c in perm_copies:
        c.wait()
    columns_of_parameters(gauss, scale, phase, col)

    def permute_spread(i):
        permute(pl.multiple_of(i * 256, 256), 256, perm0, sp, yg)
        for q in range(2):
            spread_block(1, 2 * i + q, sign, emb, h, y)
            spread_parameters(0, 2 * i + q, col, bc0)

    def permute_spread_across(i):
        permute(pl.multiple_of(D // 2 + i * 256, 256), 256, perm0, sp, yg)
        for q in range(4):
            spread_across(4 * i + q, y, sp1)
        for q in range(2):
            spread_parameters(1, 2 * i + q, col, bc1)

    loop(8, permute_spread)
    loop(8, permute_spread_across)

    both(lambda a, k: d1_copy(a, k).wait_recv())
    both(lambda a, k: d2_copy(a, k).start())

    def mix_permute(i):
        mix_across(i, yg, bc0, z)
        permute(pl.multiple_of(i * 64, 64), 64, perm1, sp1, yg1)

    def features_permute(j):
        for q in range(2):
            i = 2 * j + q
            features(0, i, (ang0, ang1)[q], bc0, fh, fl)
            permute(pl.multiple_of(16 * 64 + i * 192, 64), 192, perm1, sp1, yg1)
            (ang1, ang0)[q][...] = dot(h2, z[(i + 1) % NB])

    loop(NB, mix_permute)
    ang0[...] = dot(h2, z[0])
    loop(NB // 2, features_permute)

    loop(NB, lambda i: mix_across(i, yg1, bc1, z))

    both(lambda a, k: d2_copy(a, k).wait_recv())

    def project(a):
        part = 0.0
        for s, block in ((0, da[a]), (1, db[(a % 4) * 4 + a // 4])):
            hi, lo = split(block)
            big = dot(jnp.concatenate([hi, lo], axis=0), fh[s, a])
            part += big[:T] + (big[T:] + dot(hi, fl[s, a]))
        pacc[:T] += part

    def features_project(j):
        for q in range(2):
            i = 2 * j + q
            features(1, i, (ang0, ang1)[q], bc1, fh, fl)
            (ang1, ang0)[q][...] = dot(h2, z[(i + 1) % NB])
            project(i)

    ang0[...] = dot(h2, z[0])
    loop(NB // 2, features_project)

    def p1_copy():
        return remote(sibling, pacc, psib, p1_send, p1_recv)

    p1_copy().start()
    p1_copy().wait_recv()
    pchip[...] = pacc[...] + psib[...]

    def p2_copy(k):
        return remote(st_dev(2 * k), pchip, px.at[k], p2_send.at[k], p2_recv.at[k])

    each(4, lambda k: p2_copy(k).start())
    px[0] = pchip[...]
    each(4, lambda k: p2_copy(k).wait_recv())
    summed = (px[0] + px[1]) + (px[2] + px[3])
    projected = summed[:T]
    p_hi, p_lo = split(projected)
    p_both = jnp.concatenate([p_hi, p_lo], axis=0)

    pp_row = row_sums(jnp.square(projected))
    pp[0, :8] = jnp.concatenate([pp_row, pp_row], axis=1)
    pp[0, 8:] = summed[T:, :128]

    def pp_copy(k):
        return remote(ex_dev(0, k), pp.at[0], pp.at[k], pp_send.at[k], pp_recv.at[k])

    def pp2_copy(k):
        return remote(ex_dev(k, 0), pp2.at[0], pp2.at[k], pp2_send.at[k], pp2_recv.at[k])

    each(4, lambda k: pp_copy(k).start())

    def image(s, e):
        big = dot_t(p_both, fh[s, e])
        return big[:T] + big[T:] + dot_t(p_hi, fl[s, e])

    def i1_copy(a, near, far):
        if a:
            return remote(
                ex_dev(0, near), sa.at[near, far], ra1.at[near, far], i1_send.at[0, near, far], i1_recv.at[0, near, far]
            )
        return remote(
            ex_dev(near, 0), sb.at[near, far], rb1.at[near, far], i1_send.at[1, near, far], i1_recv.at[1, near, far]
        )

    def image_out(i):
        far, near = (i // 4 + 1) % 4, (i + 1) % 4
        sa[near, far] = image(0, ring(ez, far) * 4 + ring(ey, near))
        sb[near, far] = image(1, ring(ez, near) * 4 + ring(ey, far))

        @pl.when(near > 0)
        def _():
            i1_copy(True, near, far).start()
            i1_copy(False, near, far).start()

    each(16, image_out, 0)

    each(4, lambda k: pp_copy(k).wait())
    pp2[0] = jnp.sum(pp[...], axis=0)
    each(4, lambda k: pp2_copy(k).start())

    def i2_copy(a, k):
        if a:
            return remote(ex_dev(k, 0), sa2.at[k], ra2.at[k], i2_send.at[0, k], i2_recv.at[0, k])
        return remote(ex_dev(0, k), sb2.at[k], rb2.at[k], i2_send.at[1, k], i2_recv.at[1, k])

    def forward(far):
        for a, src, got, out in ((True, sa, ra1, sa2), (False, sb, rb1, sb2)):
            each(4, lambda near: i1_copy(a, near, far).wait_recv())
            out[far] = (src[0, far] + got[1, far]) + (got[2, far] + got[3, far])

    def forward_out(far):
        forward(far)
        i2_copy(True, far).start()
        i2_copy(False, far).start()

    each(4, forward_out)

    each(4, lambda k: pp2_copy(k).wait())
    totals = jnp.sum(pp2[...], axis=0)
    p_norm, norm_old, d_norm = totals[:8, :T], totals[8:, :T], totals[8:, T:]
    step = column(norm_old / (RIDGE * d_norm + p_norm))
    for s in range(2):
        wide[0, :, s, :] = jnp.broadcast_to(step, (T, BLK))
    step_copy = pltpu.make_async_copy(wide.at[0], step_out, out_sem.at[0])
    step_copy.start()

    forward(0)
    both(lambda a, k: i2_copy(a, k).wait_recv())
    squares = []
    for s, own, got in ((0, sa2, ra2), (1, sb2, rb2)):
        applied = RIDGE * dire[:, s, :] + ((own[0] + got[1]) + (got[2] + got[3]))
        app[:, s, :] = applied
        squares.append(jnp.square(res[:, s, :] - step * applied))
    app_copy = pltpu.make_async_copy(app, applied_out, out_sem.at[1])
    app_copy.start()
    n_row = row_sums(jnp.concatenate(squares, axis=1))
    nn[0] = jnp.concatenate([n_row, n_row], axis=1)

    def n1_copy(k):
        return remote(ex_k(k), nn.at[0], nn.at[k], n1_send.at[k], n1_recv.at[k])

    each(NB, lambda k: n1_copy(k).start())
    each(NB, lambda k: n1_copy(k).wait())
    nn2[0] = jnp.sum(nn[...], axis=0)

    def n2_copy(k):
        return remote(st_dev(k), nn2.at[0], nn2.at[k], n2_send.at[k], n2_recv.at[k])

    each(NS, lambda k: n2_copy(k).start())
    both(lambda a, k: d1_copy(a, k).wait_send())
    both(lambda a, k: d2_copy(a, k).wait_send())
    p1_copy().wait_send()
    each(4, lambda k: p2_copy(k).wait_send())

    def i1_sent(i):
        near, far = i // 4 + 1, i % 4
        i1_copy(True, near, far).wait_send()
        i1_copy(False, near, far).wait_send()

    each(12, i1_sent, 0)
    both(lambda a, k: i2_copy(a, k).wait_send())
    step_copy.wait()
    app_copy.wait()
    each(NS, lambda k: n2_copy(k).wait())
    norm_new = jnp.sum(nn2[...], axis=0)[:, :T]
    conjugacy = column(norm_new / (norm_old + EPSILON))
    for s in range(2):
        wide[1, :, s, :] = jnp.broadcast_to(conjugacy, (T, BLK))
    conj_copy = pltpu.make_async_copy(wide.at[1], conj_out, out_sem.at[2])
    conj_copy.start()
    conj_copy.wait()


def local(embeddings, sign_bits, permutation, gaussian, scaling, phases, solution, residual, direction):
    hbm = pl.BlockSpec(memory_space=pltpu.HBM)
    dma = pltpu.SemaphoreType.DMA
    vmem = pltpu.VMEM
    block, tile = (T, BLK), (8, 128)
    applied, step, conjugacy = pl.pallas_call(
        kernel,
        out_shape=[jax.ShapeDtypeStruct(direction.shape, f32)] * 3,
        in_specs=[hbm] * 8,
        out_specs=[hbm] * 3,
        scratch_shapes=[
            vmem((D, BLK), bf16),
            vmem((2, D), jnp.int32),
            vmem((2, D), f32),
            vmem((2, D), f32),
            vmem((2, D), f32),
            vmem(direction.shape, f32),
            vmem(direction.shape, f32),
            vmem((2, D), jnp.int32),
            vmem((2, D), jnp.int32),
            pltpu.SMEM((D,), jnp.int32),
            pltpu.SMEM((D,), jnp.int32),
            dma((8,)),
            dma((2,)),
            dma((3,)),
            vmem((D, BLK), f32),
            vmem((2 * D, 128), f32),
            vmem((2 * D, 128), f32),
            vmem((2 * D, 128), f32),
            vmem((2 * D, 128), f32),
            vmem((NB, 2 * BLK, BLK), bf16),
            vmem((2, NB, BLK, BLK), bf16),
            vmem((2, NB, BLK, BLK), bf16),
            vmem((D, 8), f32),
            vmem((3, D, 128), f32),
            vmem((3, D, 128), f32),
            vmem((BLK, BLK), f32),
            vmem((BLK, BLK), f32),
            vmem((NB,) + block, f32),
            vmem((NB,) + block, f32),
            vmem((T + 8, BLK), f32),
            vmem((T + 8, BLK), f32),
            vmem((T + 8, BLK), f32),
            vmem((4, T + 8, BLK), f32),
            vmem((4, 4) + block, f32),
            vmem((4, 4) + block, f32),
            vmem((4, 4) + block, f32),
            vmem((4, 4) + block, f32),
            vmem((4,) + block, f32),
            vmem((4,) + block, f32),
            vmem((4,) + block, f32),
            vmem((4,) + block, f32),
            vmem(direction.shape, f32),
            vmem((2,) + direction.shape, f32),
            vmem((4, 16, 128), f32),
            vmem((4, 16, 128), f32),
            vmem((NB,) + tile, f32),
            vmem((NS,) + tile, f32),
            dma((2, 4)), dma((2, 4)), dma((2, 4)), dma((2, 4)),
            dma, dma, dma((4,)), dma((4,)),
            dma((2, 4, 4)), dma((2, 4, 4)), dma((2, 4)), dma((2, 4)),
            dma((4,)), dma((4,)), dma((4,)), dma((4,)),
            dma((NB,)), dma((NB,)), dma((NS,)), dma((NS,)),
        ],
        compiler_params=pltpu.CompilerParams(
            collective_id=0, has_side_effects=True, vmem_limit_bytes=60 * 2**20
        ),
    )(embeddings, sign_bits, permutation, gaussian, scaling, phases, residual, direction)
    residual_next = residual - step * applied
    return solution + step * direction, residual_next, residual_next + conjugacy * direction


def solution(mesh):
    rows, stacks, blocks = P(None, "ex"), P("stk", None), P(None, "stk", "ex")
    return jax.shard_map(
        local,
        mesh=mesh,
        in_specs=(rows, stacks, stacks, stacks, stacks, stacks, blocks, blocks, blocks),
        out_specs=(blocks, blocks, blocks),
        check_vma=False,
    )
```

```python
import functools
import math

import jax
import jax.numpy as jnp
from jax import lax
from jax.experimental import pallas as pl
from jax.experimental.pallas import tpu as pltpu
from jax.sharding import PartitionSpec as P

f32, bf16 = jnp.float32, jnp.bfloat16
MESH = pl.DeviceIdType.MESH

D = 4096
BLK = 256
NB = 16
NS = 8
T = 64
RIDGE = 0.25
EPSILON = 1e-06
TURN = 1.0 / (2.0 * math.pi)
NORM = math.sqrt(2.0 / (16 * D))
SINE = (6.283164044251588, -41.337142364570006, 81.34076867837481, -70.99343135659183)
COEF = tuple(c * NORM for c in SINE)


def hadamard():
    i = lax.broadcasted_iota(jnp.int32, (BLK, BLK), 0)
    j = lax.broadcasted_iota(jnp.int32, (BLK, BLK), 1)
    v = i & j
    v = v ^ (v >> 4)
    v = v ^ (v >> 2)
    v = v ^ (v >> 1)
    return (1 - 2 * (v & 1)).astype(f32)


def butterfly(values):
    v = list(values)
    h = 1
    while h < len(v):
        for i in range(0, len(v), 2 * h):
            for k in range(i, i + h):
                v[k], v[k + h] = v[k] + v[k + h], v[k] - v[k + h]
        h *= 2
    return v


def split(x):
    hi = x.astype(bf16)
    return hi, (x - hi.astype(f32)).astype(bf16)


def dot(a, b):
    return jnp.dot(a, b, preferred_element_type=f32)


def dot_t(a, b):
    return lax.dot_general(a, b, (((1,), (1,)), ((), ())), preferred_element_type=f32)


def row_sums(x):
    hi, lo = split(x)
    ones = jnp.ones((8, x.shape[1]), bf16)
    return dot_t(ones, hi) + dot_t(ones, lo)


def column(row):
    wide = jnp.concatenate([row, row], axis=1)
    return jnp.transpose(wide)[:T, 0:1]


def columns_of_parameters(gauss, scale, phase, col):
    for b in range(D // 128):
        at = slice(b * 128, (b + 1) * 128)
        block = jnp.concatenate(
            [
                gauss[:, at],
                scale[:, at] * (TURN / D),
                phase[:, at] * TURN,
                jnp.zeros((2, 128), f32),
            ],
            axis=0,
        )
        col[at, :] = jnp.transpose(block)


def spread_block(s, a, sign, emb, h, y):
    o = pl.multiple_of(a * BLK, BLK)
    signs = (2 * sign[s : s + 1, pl.ds(o, BLK)] - 1).astype(f32)
    y[pl.ds(o, BLK), :] = dot((h * signs).astype(bf16), emb[pl.ds(o, BLK), :])


def spread_across(r, y, sp):
    o = pl.multiple_of(r * 8, 8)
    for half in range(2):
        lanes = slice(half * 128, (half + 1) * 128)
        v = butterfly([y[pl.ds(a * BLK + o, 8), lanes] for a in range(NB)])
        for a in range(NB):
            sp[pl.ds(2 * (a * BLK + o) + half, 8, stride=2), :] = v[a]


def permute(base, rows, perm, sp, yg):
    out = yg.at[pl.ds(pl.multiple_of(2 * base, 2 * 8), 2 * rows)]
    for k in range(rows):
        out[2 * k : 2 * k + 2, :] = sp[pl.ds(perm[base + k], 2), :]


def mix_across(r, yg, bc, z):
    o = pl.multiple_of(r * 16, 16)
    for half in range(2):
        lanes = slice(half * 128, (half + 1) * 128)
        v = butterfly(
            [
                yg[pl.ds(2 * (a * BLK + o) + half, 16, stride=2), :] * bc[0, pl.ds(a * BLK + o, 16), :]
                for a in range(NB)
            ]
        )
        for a in range(NB):
            hi, lo = split(v[a])
            z[a, pl.ds(o, 16), lanes] = hi
            z[a, pl.ds(BLK + o, 16), lanes] = lo


def loop(n, f, unroll=1):
    def body(i, _):
        f(i)
        return 0

    lax.fori_loop(0, n, body, 0, unroll=unroll)


def cosine(turns):
    x = 0.25 - jnp.abs(turns - jnp.round(turns))
    u = x * x
    p = COEF[3]
    for c in COEF[2::-1]:
        p = p * u + c
    return p * x


def spread_parameters(s, a, col, bc):
    at = pl.ds(pl.multiple_of(a * BLK, BLK), BLK)
    for v in range(3):
        bc[v, at, :] = jnp.broadcast_to(col[at, 2 * v + s : 2 * v + s + 1], (BLK, 128))


def features(s, a, ang, bc, fh, fl, also=None):
    o = pl.multiple_of(a * BLK, BLK)
    for c in range(8):
        rows = slice(c * 32, (c + 1) * 32)
        at = pl.ds(o + c * 32, 32)
        for half in range(2):
            lanes = slice(half * 128, (half + 1) * 128)
            hi, lo = split(cosine(ang[rows, lanes] * bc[1, at, :] + bc[2, at, :]))
            fh[s, a, rows, lanes] = hi
            fl[s, a, rows, lanes] = lo
        if also is not None:
            also(c)


def kernel(
    emb_h, sign_h, perm_h, gauss_h, scale_h, phase_h, res_h, dire_h,
    applied_out, step_out, conj_out,
    emb, sign, gauss, scale, phase, res, dire, pv, pv2, perm0, perm1, in_sem, perm_sem, out_sem,
    y, sp, yg, sp1, yg1, z, fh, fl, col, bc0, bc1, ang0, ang1,
    da, db, pacc, psib, pchip, px, sa, sb, ra1, rb1, sa2, sb2, ra2, rb2, app, wide, pp, pp2, nn, nn2,
    d1_send, d1_recv, d2_send, d2_recv,
    p1_send, p1_recv, p2_send, p2_recv, i1_send, i1_recv, i2_send, i2_recv,
    pp_send, pp_recv, pp2_send, pp2_recv, n1_send, n1_recv, n2_send, n2_recv,
):
    ex = lax.axis_index("ex")
    st = lax.axis_index("stk")
    ez, ey = ex // 4, ex % 4

    def ring(i, k):
        return (i + k) % 4

    def ex_dev(dz, dy):
        return (ring(ez, dz) * 4 + ring(ey, dy), st)

    def st_dev(k):
        return (ex, (st + k) % NS)

    sibling = (ex, st + 1 - 2 * (st % 2))

    def remote(dev, src, dst, send, recv):
        return pltpu.make_async_remote_copy(
            src_ref=src, dst_ref=dst, send_sem=send, recv_sem=recv, device_id=dev, device_id_type=MESH
        )

    def each(n, f, first=1):
        def body(k, _):
            f(k)
            return 0

        lax.fori_loop(first, n, body, 0)

    def ex_k(k):
        return ex_dev(k // 4, k % 4)

    inputs = [
        pltpu.make_async_copy(src, dst, in_sem.at[i])
        for i, (src, dst) in enumerate(
            [
                (dire_h, dire), (res_h, res), (sign_h, sign), (emb_h, emb), (gauss_h, gauss),
                (scale_h, scale), (phase_h, phase), (perm_h, pv),
            ]
        )
    ]
    for c in inputs:
        c.start()
    barrier = pltpu.get_barrier_semaphore()
    each(NB, lambda k: pl.semaphore_signal(barrier, inc=1, device_id=ex_k(k), device_id_type=MESH))
    each(NS, lambda k: pl.semaphore_signal(barrier, inc=1, device_id=st_dev(k), device_id_type=MESH))

    h = hadamard()
    hb = h.astype(bf16)
    h2 = jnp.concatenate([hb, hb], axis=1)

    inputs[0].wait()
    inputs[1].wait()
    own_a, own_b = ex, ey * 4 + ez
    da[own_a] = dire[:, 0, :]
    db[own_b] = dire[:, 1, :]

    inputs[7].wait()
    pv2[...] = 2 * pv[...]
    perm_copies = [
        pltpu.make_async_copy(pv2.at[s], p, perm_sem.at[s]) for s, p in enumerate((perm0, perm1))
    ]
    for c in perm_copies:
        c.start()
    inputs[2].wait()
    inputs[3].wait()
    loop(NB, lambda a: spread_block(0, a, sign, emb, h, y), 4)
    loop(32, lambda r: spread_across(r, y, sp), 2)

    r2 = row_sums(jnp.concatenate([jnp.square(res[:, s, :]) for s in range(2)], axis=1))
    d2 = row_sums(jnp.concatenate([jnp.square(dire[:, s, :]) for s in range(2)], axis=1))
    pacc[...] = jnp.zeros_like(pacc)
    pacc[T:, :128] = jnp.concatenate([r2, d2], axis=1)

    for i in (4, 5, 6):
        inputs[i].wait()
    for c in perm_copies:
        c.wait()
    columns_of_parameters(gauss, scale, phase, col)

    def permute_spread(i):
        permute(pl.multiple_of(i * 256, 256), 256, perm0, sp, yg)
        for q in range(2):
            spread_block(1, 2 * i + q, sign, emb, h, y)
            spread_parameters(0, 2 * i + q, col, bc0)

    def permute_spread_across(i):
        permute(pl.multiple_of(D // 2 + i * 256, 256), 256, perm0, sp, yg)
        for q in range(4):
            spread_across(4 * i + q, y, sp1)
        for q in range(2):
            spread_parameters(1, 2 * i + q, col, bc1)

    loop(3, permute_spread)
    pl.semaphore_wait(barrier, NB - 1 + NS - 1)
    def d1_copy(a, k):
        if a:
            return remote(ex_dev(0, k), da.at[own_a], da.at[own_a], d1_send.at[0, k], d1_recv.at[0, k])
        return remote(ex_dev(k, 0), db.at[own_b], db.at[own_b], d1_send.at[1, k], d1_recv.at[1, k])

    def d2_copy(a, k):
        four_a, four_b = da.at[pl.ds(ez * 4, 4)], db.at[pl.ds(ey * 4, 4)]
        if a:
            return remote(ex_dev(k, 0), four_a, four_a, d2_send.at[0, k], d2_recv.at[0, k])
        return remote(ex_dev(0, k), four_b, four_b, d2_send.at[1, k], d2_recv.at[1, k])

    def both(f):
        def go(k):
            f(True, k)
            f(False, k)

        each(4, go)

    both(lambda a, k: d1_copy(a, k).start())

    loop(8 - 3, lambda i: permute_spread(3 + i))
    both(lambda a, k: d1_copy(a, k).wait_recv())
    both(lambda a, k: d2_copy(a, k).start())
    loop(8, permute_spread_across)

    def mix_permute(i):
        mix_across(i, yg, bc0, z)
        permute(pl.multiple_of(i * 64, 64), 64, perm1, sp1, yg1)

    def features_permute(j):
        for q in range(2):
            i = 2 * j + q
            features(0, i, (ang0, ang1)[q], bc0, fh, fl)
            permute(pl.multiple_of(16 * 64 + i * 192, 64), 192, perm1, sp1, yg1)
            (ang1, ang0)[q][...] = dot(h2, z[(i + 1) % NB])

    loop(NB, mix_permute)
    ang0[...] = dot(h2, z[0])
    loop(NB // 2, features_permute)

    loop(NB, lambda i: mix_across(i, yg1, bc1, z))

    def project(a):
        part = 0.0
        for s, block in ((0, da[a]), (1, db[(a % 4) * 4 + a // 4])):
            hi, lo = split(block)
            big = dot(jnp.concatenate([hi, lo], axis=0), fh[s, a])
            part += big[:T] + (big[T:] + dot(hi, fl[s, a]))
        pacc[:T] += part

    def features_project(j):
        for q in range(2):
            i = 2 * j + q
            features(1, i, (ang0, ang1)[q], bc1, fh, fl)
            (ang1, ang0)[q][...] = dot(h2, z[(i + 1) % NB])
            project(i)

    ang0[...] = dot(h2, z[0])
    both(lambda a, k: d2_copy(a, k).wait_recv())
    loop(NB // 2, features_project)

    def p1_copy():
        return remote(sibling, pacc, psib, p1_send, p1_recv)

    p1_copy().start()
    p1_copy().wait_recv()
    pchip[...] = pacc[...] + psib[...]

    def p2_copy(k):
        return remote(st_dev(2 * k), pchip, px.at[k], p2_send.at[k], p2_recv.at[k])

    each(4, lambda k: p2_copy(k).start())
    px[0] = pchip[...]
    each(4, lambda k: p2_copy(k).wait_recv())
    summed = (px[0] + px[1]) + (px[2] + px[3])
    projected = summed[:T]
    p_hi, p_lo = split(projected)
    p_both = jnp.concatenate([p_hi, p_lo], axis=0)

    pp_row = row_sums(jnp.square(projected))
    pp[0, :8] = jnp.concatenate([pp_row, pp_row], axis=1)
    pp[0, 8:] = summed[T:, :128]

    def pp_copy(k):
        return remote(ex_dev(0, k), pp.at[0], pp.at[k], pp_send.at[k], pp_recv.at[k])

    def pp2_copy(k):
        return remote(ex_dev(k, 0), pp2.at[0], pp2.at[k], pp2_send.at[k], pp2_recv.at[k])

    each(4, lambda k: pp_copy(k).start())

    def image(s, e):
        big = dot_t(p_both, fh[s, e])
        return big[:T] + big[T:] + dot_t(p_hi, fl[s, e])

    def i1_copy(a, near, far):
        if a:
            return remote(
                ex_dev(0, near), sa.at[near, far], ra1.at[near, far], i1_send.at[0, near, far], i1_recv.at[0, near, far]
            )
        return remote(
            ex_dev(near, 0), sb.at[near, far], rb1.at[near, far], i1_send.at[1, near, far], i1_recv.at[1, near, far]
        )

    def image_out(i):
        far, near = (i // 4 + 1) % 4, (i + 1) % 4
        sa[near, far] = image(0, ring(ez, far) * 4 + ring(ey, near))
        sb[near, far] = image(1, ring(ez, near) * 4 + ring(ey, far))

        @pl.when(near > 0)
        def _():
            i1_copy(True, near, far).start()
            i1_copy(False, near, far).start()

    each(16, image_out, 0)

    each(4, lambda k: pp_copy(k).wait())
    pp2[0] = jnp.sum(pp[...], axis=0)
    each(4, lambda k: pp2_copy(k).start())

    def i2_copy(a, k):
        if a:
            return remote(ex_dev(k, 0), sa2.at[k], ra2.at[k], i2_send.at[0, k], i2_recv.at[0, k])
        return remote(ex_dev(0, k), sb2.at[k], rb2.at[k], i2_send.at[1, k], i2_recv.at[1, k])

    def forward(far):
        for a, src, got, out in ((True, sa, ra1, sa2), (False, sb, rb1, sb2)):
            each(4, lambda near: i1_copy(a, near, far).wait_recv())
            out[far] = (src[0, far] + got[1, far]) + (got[2, far] + got[3, far])

    def forward_out(far):
        forward(far)
        i2_copy(True, far).start()
        i2_copy(False, far).start()

    each(4, forward_out)

    each(4, lambda k: pp2_copy(k).wait())
    totals = jnp.sum(pp2[...], axis=0)
    p_norm, norm_old, d_norm = totals[:8, :T], totals[8:, :T], totals[8:, T:]
    step = column(norm_old / (RIDGE * d_norm + p_norm))
    for s in range(2):
        wide[0, :, s, :] = jnp.broadcast_to(step, (T, BLK))
    step_copy = pltpu.make_async_copy(wide.at[0], step_out, out_sem.at[0])
    step_copy.start()

    forward(0)
    both(lambda a, k: i2_copy(a, k).wait_recv())
    squares = []
    for s, own, got in ((0, sa2, ra2), (1, sb2, rb2)):
        applied = RIDGE * dire[:, s, :] + ((own[0] + got[1]) + (got[2] + got[3]))
        app[:, s, :] = applied
        squares.append(jnp.square(res[:, s, :] - step * applied))
    app_copy = pltpu.make_async_copy(app, applied_out, out_sem.at[1])
    app_copy.start()
    n_row = row_sums(jnp.concatenate(squares, axis=1))
    nn[0] = jnp.concatenate([n_row, n_row], axis=1)

    def n1_copy(k):
        return remote(ex_k(k), nn.at[0], nn.at[k], n1_send.at[k], n1_recv.at[k])

    for k in (10, 9, 11, 6, 14, 8, 2, 5, 7, 13, 15, 1, 3, 4, 12):
        n1_copy(k).start()
    each(NB, lambda k: n1_copy(k).wait())
    nn2[0] = jnp.sum(nn[...], axis=0)

    def n2_copy(k):
        return remote(st_dev(k), nn2.at[0], nn2.at[k], n2_send.at[k], n2_recv.at[k])

    for k in (4, 5, 3, 2, 6, 7, 1):
        n2_copy(k).start()
    both(lambda a, k: d1_copy(a, k).wait_send())
    both(lambda a, k: d2_copy(a, k).wait_send())
    p1_copy().wait_send()
    each(4, lambda k: p2_copy(k).wait_send())

    def i1_sent(i):
        near, far = i // 4 + 1, i % 4
        i1_copy(True, near, far).wait_send()
        i1_copy(False, near, far).wait_send()

    each(12, i1_sent, 0)
    both(lambda a, k: i2_copy(a, k).wait_send())
    step_copy.wait()
    app_copy.wait()
    each(NS, lambda k: n2_copy(k).wait())
    norm_new = jnp.sum(nn2[...], axis=0)[:, :T]
    conjugacy = column(norm_new / (norm_old + EPSILON))
    for s in range(2):
        wide[1, :, s, :] = jnp.broadcast_to(conjugacy, (T, BLK))
    conj_copy = pltpu.make_async_copy(wide.at[1], conj_out, out_sem.at[2])
    conj_copy.start()
    conj_copy.wait()


def local(embeddings, sign_bits, permutation, gaussian, scaling, phases, solution, residual, direction):
    hbm = pl.BlockSpec(memory_space=pltpu.HBM)
    dma = pltpu.SemaphoreType.DMA
    vmem = pltpu.VMEM
    block, tile = (T, BLK), (8, 128)
    applied, step, conjugacy = pl.pallas_call(
        kernel,
        out_shape=[jax.ShapeDtypeStruct(direction.shape, f32)] * 3,
        in_specs=[hbm] * 8,
        out_specs=[hbm] * 3,
        scratch_shapes=[
            vmem((D, BLK), bf16),
            vmem((2, D), jnp.int32),
            vmem((2, D), f32),
            vmem((2, D), f32),
            vmem((2, D), f32),
            vmem(direction.shape, f32),
            vmem(direction.shape, f32),
            vmem((2, D), jnp.int32),
            vmem((2, D), jnp.int32),
            pltpu.SMEM((D,), jnp.int32),
            pltpu.SMEM((D,), jnp.int32),
            dma((8,)),
            dma((2,)),
            dma((3,)),
            vmem((D, BLK), f32),
            vmem((2 * D, 128), f32),
            vmem((2 * D, 128), f32),
            vmem((2 * D, 128), f32),
            vmem((2 * D, 128), f32),
            vmem((NB, 2 * BLK, BLK), bf16),
            vmem((2, NB, BLK, BLK), bf16),
            vmem((2, NB, BLK, BLK), bf16),
            vmem((D, 8), f32),
            vmem((3, D, 128), f32),
            vmem((3, D, 128), f32),
            vmem((BLK, BLK), f32),
            vmem((BLK, BLK), f32),
            vmem((NB,) + block, f32),
            vmem((NB,) + block, f32),
            vmem((T + 8, BLK), f32),
            vmem((T + 8, BLK), f32),
            vmem((T + 8, BLK), f32),
            vmem((4, T + 8, BLK), f32),
            vmem((4, 4) + block, f32),
            vmem((4, 4) + block, f32),
            vmem((4, 4) + block, f32),
            vmem((4, 4) + block, f32),
            vmem((4,) + block, f32),
            vmem((4,) + block, f32),
            vmem((4,) + block, f32),
            vmem((4,) + block, f32),
            vmem(direction.shape, f32),
            vmem((2,) + direction.shape, f32),
            vmem((4, 16, 128), f32),
            vmem((4, 16, 128), f32),
            vmem((NB,) + tile, f32),
            vmem((NS,) + tile, f32),
            dma((2, 4)), dma((2, 4)), dma((2, 4)), dma((2, 4)),
            dma, dma, dma((4,)), dma((4,)),
            dma((2, 4, 4)), dma((2, 4, 4)), dma((2, 4)), dma((2, 4)),
            dma((4,)), dma((4,)), dma((4,)), dma((4,)),
            dma((NB,)), dma((NB,)), dma((NS,)), dma((NS,)),
        ],
        compiler_params=pltpu.CompilerParams(
            collective_id=0, has_side_effects=True, vmem_limit_bytes=60 * 2**20
        ),
    )(embeddings, sign_bits, permutation, gaussian, scaling, phases, residual, direction)
    residual_next = residual - step * applied
    return solution + step * direction, residual_next, residual_next + conjugacy * direction


def solution(mesh):
    rows, stacks, blocks = P(None, "ex"), P("stk", None), P(None, "stk", "ex")
    return jax.shard_map(
        local,
        mesh=mesh,
        in_specs=(rows, stacks, stacks, stacks, stacks, stacks, blocks, blocks, blocks),
        out_specs=(blocks, blocks, blocks),
        check_vma=False,
    )
```

```python
import functools
import math

import jax
import jax.numpy as jnp
from jax import lax
from jax.experimental import pallas as pl
from jax.experimental.pallas import tpu as pltpu
from jax.sharding import PartitionSpec as P

f32, bf16 = jnp.float32, jnp.bfloat16
MESH = pl.DeviceIdType.MESH

D = 4096
BLK = 256
NB = 16
NS = 8
T = 64
RIDGE = 0.25
EPSILON = 1e-06
TURN = 1.0 / (2.0 * math.pi)
NORM = math.sqrt(2.0 / (16 * D))
SINE = (6.283164044251588, -41.337142364570006, 81.34076867837481, -70.99343135659183)
COEF = tuple(c * NORM for c in SINE)


def hadamard():
    i = lax.broadcasted_iota(jnp.int32, (BLK, BLK), 0)
    j = lax.broadcasted_iota(jnp.int32, (BLK, BLK), 1)
    v = i & j
    v = v ^ (v >> 4)
    v = v ^ (v >> 2)
    v = v ^ (v >> 1)
    return (1 - 2 * (v & 1)).astype(f32)


def butterfly(values):
    v = list(values)
    h = 1
    while h < len(v):
        for i in range(0, len(v), 2 * h):
            for k in range(i, i + h):
                v[k], v[k + h] = v[k] + v[k + h], v[k] - v[k + h]
        h *= 2
    return v


def split(x):
    hi = x.astype(bf16)
    return hi, (x - hi.astype(f32)).astype(bf16)


def dot(a, b):
    return jnp.dot(a, b, preferred_element_type=f32)


def dot_t(a, b):
    return lax.dot_general(a, b, (((1,), (1,)), ((), ())), preferred_element_type=f32)


def row_sums(x):
    hi, lo = split(x)
    ones = jnp.ones((8, x.shape[1]), bf16)
    return dot_t(ones, hi) + dot_t(ones, lo)


def column(row):
    wide = jnp.concatenate([row, row], axis=1)
    return jnp.transpose(wide)[:T, 0:1]


def columns_of_parameters(gauss, scale, phase, col):
    for b in range(D // 128):
        at = slice(b * 128, (b + 1) * 128)
        block = jnp.concatenate(
            [
                gauss[:, at],
                scale[:, at] * (TURN / D),
                phase[:, at] * TURN,
                jnp.zeros((2, 128), f32),
            ],
            axis=0,
        )
        col[at, :] = jnp.transpose(block)


def spread_block(s, a, sign, emb, h, y):
    o = pl.multiple_of(a * BLK, BLK)
    signs = (2 * sign[s : s + 1, pl.ds(o, BLK)] - 1).astype(f32)
    y[pl.ds(o, BLK), :] = dot((h * signs).astype(bf16), emb[pl.ds(o, BLK), :])


def spread_across(r, y, sp):
    o = pl.multiple_of(r * 8, 8)
    for half in range(2):
        lanes = slice(half * 128, (half + 1) * 128)
        v = butterfly([y[pl.ds(a * BLK + o, 8), lanes] for a in range(NB)])
        for a in range(NB):
            sp[pl.ds(2 * (a * BLK + o) + half, 8, stride=2), :] = v[a]


def permute(base, rows, perm, sp, yg):
    out = yg.at[pl.ds(pl.multiple_of(2 * base, 2 * 8), 2 * rows)]
    for k in range(rows):
        out[2 * k : 2 * k + 2, :] = sp[pl.ds(perm[base + k], 2), :]


def mix_across(r, yg, bc, z):
    o = pl.multiple_of(r * 16, 16)
    for half in range(2):
        lanes = slice(half * 128, (half + 1) * 128)
        v = butterfly(
            [
                yg[pl.ds(2 * (a * BLK + o) + half, 16, stride=2), :] * bc[0, pl.ds(a * BLK + o, 16), :]
                for a in range(NB)
            ]
        )
        for a in range(NB):
            hi, lo = split(v[a])
            z[a, pl.ds(o, 16), lanes] = hi
            z[a, pl.ds(BLK + o, 16), lanes] = lo


def loop(n, f, unroll=1):
    def body(i, _):
        f(i)
        return 0

    lax.fori_loop(0, n, body, 0, unroll=unroll)


def cosine(turns):
    x = 0.25 - jnp.abs(turns - jnp.round(turns))
    u = x * x
    p = COEF[3]
    for c in COEF[2::-1]:
        p = p * u + c
    return p * x


def spread_parameters(s, a, col, bc):
    at = pl.ds(pl.multiple_of(a * BLK, BLK), BLK)
    for v in range(3):
        bc[v, at, :] = jnp.broadcast_to(col[at, 2 * v + s : 2 * v + s + 1], (BLK, 128))


def features(s, a, ang, bc, fh, fl, also=None):
    o = pl.multiple_of(a * BLK, BLK)
    for c in range(8):
        rows = slice(c * 32, (c + 1) * 32)
        at = pl.ds(o + c * 32, 32)
        for half in range(2):
            lanes = slice(half * 128, (half + 1) * 128)
            hi, lo = split(cosine(ang[rows, lanes] * bc[1, at, :] + bc[2, at, :]))
            fh[s, a, rows, lanes] = hi
            fl[s, a, rows, lanes] = lo
        if also is not None:
            also(c)


def kernel(
    emb_h, sign_h, perm_h, gauss_h, scale_h, phase_h, res_h, dire_h,
    applied_out, step_out, conj_out,
    emb, sign, gauss, scale, phase, res, dire, pv, pv2, perm0, perm1, in_sem, perm_sem, out_sem,
    y, sp, yg, sp1, yg1, z, fh, fl, col, bc0, bc1, ang0, ang1,
    da, db, pacc, psib, pchip, px, sa, sb, ra1, rb1, relay, sa2, sb2, ra2, rb2, app, wide, pp, pp2, nn, nn2,
    d1_send, d1_recv, d2_send, d2_recv,
    p1_send, p1_recv, p2_send, p2_recv, i1_send, i1_recv, i2_send, i2_recv, r_send, r_recv,
    pp_send, pp_recv, pp2_send, pp2_recv, n1_send, n1_recv, n2_send, n2_recv,
):
    ex = lax.axis_index("ex")
    st = lax.axis_index("stk")
    ez, ey = ex // 4, ex % 4

    def ring(i, k):
        return (i + k) % 4

    def ex_dev(dz, dy):
        return (ring(ez, dz) * 4 + ring(ey, dy), st)

    def st_dev(k):
        return (ex, (st + k) % NS)

    sibling = (ex, st + 1 - 2 * (st % 2))

    def remote(dev, src, dst, send, recv):
        return pltpu.make_async_remote_copy(
            src_ref=src, dst_ref=dst, send_sem=send, recv_sem=recv, device_id=dev, device_id_type=MESH
        )

    def each(n, f, first=1):
        def body(k, _):
            f(k)
            return 0

        lax.fori_loop(first, n, body, 0)

    def ex_k(k):
        return ex_dev(k // 4, k % 4)

    inputs = [
        pltpu.make_async_copy(src, dst, in_sem.at[i])
        for i, (src, dst) in enumerate(
            [
                (dire_h, dire), (res_h, res), (sign_h, sign), (emb_h, emb), (gauss_h, gauss),
                (scale_h, scale), (phase_h, phase), (perm_h, pv),
            ]
        )
    ]
    for c in inputs:
        c.start()
    barrier = pltpu.get_barrier_semaphore()
    each(NB, lambda k: pl.semaphore_signal(barrier, inc=1, device_id=ex_k(k), device_id_type=MESH))
    each(NS, lambda k: pl.semaphore_signal(barrier, inc=1, device_id=st_dev(k), device_id_type=MESH))

    h = hadamard()
    hb = h.astype(bf16)
    h2 = jnp.concatenate([hb, hb], axis=1)

    inputs[0].wait()
    inputs[1].wait()
    own_a, own_b = ex, ey * 4 + ez
    da[own_a] = dire[:, 0, :]
    db[own_b] = dire[:, 1, :]

    inputs[7].wait()
    pv2[...] = 2 * pv[...]
    perm_copies = [
        pltpu.make_async_copy(pv2.at[s], p, perm_sem.at[s]) for s, p in enumerate((perm0, perm1))
    ]
    for c in perm_copies:
        c.start()
    inputs[2].wait()
    inputs[3].wait()
    loop(NB, lambda a: spread_block(0, a, sign, emb, h, y), 4)
    loop(32, lambda r: spread_across(r, y, sp), 2)

    r2 = row_sums(jnp.concatenate([jnp.square(res[:, s, :]) for s in range(2)], axis=1))
    d2 = row_sums(jnp.concatenate([jnp.square(dire[:, s, :]) for s in range(2)], axis=1))
    pacc[...] = jnp.zeros_like(pacc)
    pacc[T:, :128] = jnp.concatenate([r2, d2], axis=1)

    for i in (4, 5, 6):
        inputs[i].wait()
    for c in perm_copies:
        c.wait()
    columns_of_parameters(gauss, scale, phase, col)

    def permute_spread(i):
        permute(pl.multiple_of(i * 256, 256), 256, perm0, sp, yg)
        for q in range(2):
            spread_block(1, 2 * i + q, sign, emb, h, y)
            spread_parameters(0, 2 * i + q, col, bc0)

    def permute_spread_across(i):
        permute(pl.multiple_of(D // 2 + i * 256, 256), 256, perm0, sp, yg)
        for q in range(4):
            spread_across(4 * i + q, y, sp1)
        for q in range(2):
            spread_parameters(1, 2 * i + q, col, bc1)

    loop(3, permute_spread)
    pl.semaphore_wait(barrier, NB - 1 + NS - 1)
    def d1_copy(a, k):
        if a:
            return remote(ex_dev(0, k), da.at[own_a], da.at[own_a], d1_send.at[0, k], d1_recv.at[0, k])
        return remote(ex_dev(k, 0), db.at[own_b], db.at[own_b], d1_send.at[1, k], d1_recv.at[1, k])

    def d2_copy(a, k):
        four_a, four_b = da.at[pl.ds(ez * 4, 4)], db.at[pl.ds(ey * 4, 4)]
        if a:
            return remote(ex_dev(k, 0), four_a, four_a, d2_send.at[0, k], d2_recv.at[0, k])
        return remote(ex_dev(0, k), four_b, four_b, d2_send.at[1, k], d2_recv.at[1, k])

    def both(f):
        def go(k):
            f(True, k)
            f(False, k)

        each(4, go)

    both(lambda a, k: d1_copy(a, k).start())

    loop(8 - 3, lambda i: permute_spread(3 + i))
    both(lambda a, k: d1_copy(a, k).wait_recv())
    both(lambda a, k: d2_copy(a, k).start())
    loop(8, permute_spread_across)

    def mix_permute(i):
        mix_across(i, yg, bc0, z)
        permute(pl.multiple_of(i * 64, 64), 64, perm1, sp1, yg1)

    def features_permute(j):
        for q in range(2):
            i = 2 * j + q
            features(0, i, (ang0, ang1)[q], bc0, fh, fl)
            permute(pl.multiple_of(16 * 64 + i * 192, 64), 192, perm1, sp1, yg1)
            (ang1, ang0)[q][...] = dot(h2, z[(i + 1) % NB])

    loop(NB, mix_permute)
    ang0[...] = dot(h2, z[0])
    loop(NB // 2, features_permute)

    loop(NB, lambda i: mix_across(i, yg1, bc1, z))

    def project(a):
        part = 0.0
        for s, block in ((0, da[a]), (1, db[(a % 4) * 4 + a // 4])):
            hi, lo = split(block)
            big = dot(jnp.concatenate([hi, lo], axis=0), fh[s, a])
            part += big[:T] + (big[T:] + dot(hi, fl[s, a]))
        pacc[:T] += part

    def features_project(j):
        for q in range(2):
            i = 2 * j + q
            features(1, i, (ang0, ang1)[q], bc1, fh, fl)
            (ang1, ang0)[q][...] = dot(h2, z[(i + 1) % NB])
            project(i)

    ang0[...] = dot(h2, z[0])
    both(lambda a, k: d2_copy(a, k).wait_recv())
    loop(NB // 2, features_project)

    def p1_copy():
        return remote(sibling, pacc, psib, p1_send, p1_recv)

    p1_copy().start()
    p1_copy().wait_recv()
    pchip[...] = pacc[...] + psib[...]

    def p2_copy(k):
        return remote(st_dev(2 * k), pchip, px.at[k], p2_send.at[k], p2_recv.at[k])

    each(4, lambda k: p2_copy(k).start())
    px[0] = pchip[...]
    each(4, lambda k: p2_copy(k).wait_recv())
    summed = (px[0] + px[1]) + (px[2] + px[3])
    projected = summed[:T]
    p_hi, p_lo = split(projected)
    p_both = jnp.concatenate([p_hi, p_lo], axis=0)

    pp_row = row_sums(jnp.square(projected))
    pp[0, :8] = jnp.concatenate([pp_row, pp_row], axis=1)
    pp[0, 8:] = summed[T:, :128]

    def pp_copy(k):
        return remote(ex_dev(0, k), pp.at[0], pp.at[k], pp_send.at[k], pp_recv.at[k])

    def pp2_copy(k):
        return remote(ex_dev(k, 0), pp2.at[0], pp2.at[k], pp2_send.at[k], pp2_recv.at[k])

    each(4, lambda k: pp_copy(k).start())

    def image(s, e):
        big = dot_t(p_both, fh[s, e])
        return big[:T] + big[T:] + dot_t(p_hi, fl[s, e])

    def i1_copy(a, near, far):
        if a:
            return remote(
                ex_dev(0, near), sa.at[near, far], ra1.at[near, far], i1_send.at[0, near, far], i1_recv.at[0, near, far]
            )
        return remote(
            ex_dev(near, 0), sb.at[near, far], rb1.at[near, far], i1_send.at[1, near, far], i1_recv.at[1, near, far]
        )

    def via(far):
        return 1 + 2 * (far % 2)

    def relay_copy(a, far):
        if a:
            return remote(ex_dev(0, via(far)), sa.at[2, far], relay.at[0, far], r_send.at[0, far], r_recv.at[0, far])
        return remote(ex_dev(via(far), 0), sb.at[2, far], relay.at[1, far], r_send.at[1, far], r_recv.at[1, far])

    def images(near, far):
        sa[near, far] = image(0, ring(ez, far) * 4 + ring(ey, near))
        sb[near, far] = image(1, ring(ez, near) * 4 + ring(ey, far))

    def start_images(near, far):
        i1_copy(True, near, far).start()
        i1_copy(False, near, far).start()

    def opposite(i):
        far = (i + 1) % 4
        images(2, far)
        relay_copy(True, far).start()
        relay_copy(False, far).start()

    def direct(i):
        far = (i + 1) % 4
        images(4 - via(far), far)
        start_images(4 - via(far), far)

    def relayed(i):
        far = (i + 1) % 4
        relay_copy(True, far).wait_recv()
        relay_copy(False, far).wait_recv()
        sa[via(far), far] += relay[0, far]
        sb[via(far), far] += relay[1, far]
        start_images(via(far), far)

    each(4, opposite, 0)
    each(4, direct, 0)
    each(4, lambda i: images(via((i + 1) % 4), (i + 1) % 4), 0)
    each(4, relayed, 0)
    each(4, lambda far: images(0, far), 0)

    each(4, lambda k: pp_copy(k).wait())
    pp2[0] = jnp.sum(pp[...], axis=0)
    each(4, lambda k: pp2_copy(k).start())

    def i2_copy(a, k):
        if a:
            return remote(ex_dev(k, 0), sa2.at[k], ra2.at[k], i2_send.at[0, k], i2_recv.at[0, k])
        return remote(ex_dev(0, k), sb2.at[k], rb2.at[k], i2_send.at[1, k], i2_recv.at[1, k])

    def forward(far):
        for a, src, got, out in ((True, sa, ra1, sa2), (False, sb, rb1, sb2)):
            i1_copy(a, 1, far).wait_recv()
            i1_copy(a, 3, far).wait_recv()
            out[far] = src[0, far] + (got[1, far] + got[3, far])

    def forward_out(far):
        forward(far)
        i2_copy(True, far).start()
        i2_copy(False, far).start()

    each(4, forward_out)

    each(4, lambda k: pp2_copy(k).wait())
    totals = jnp.sum(pp2[...], axis=0)
    p_norm, norm_old, d_norm = totals[:8, :T], totals[8:, :T], totals[8:, T:]
    step = column(norm_old / (RIDGE * d_norm + p_norm))
    for s in range(2):
        wide[0, :, s, :] = jnp.broadcast_to(step, (T, BLK))
    step_copy = pltpu.make_async_copy(wide.at[0], step_out, out_sem.at[0])
    step_copy.start()

    forward(0)
    both(lambda a, k: i2_copy(a, k).wait_recv())
    squares = []
    for s, own, got in ((0, sa2, ra2), (1, sb2, rb2)):
        applied = RIDGE * dire[:, s, :] + ((own[0] + got[1]) + (got[2] + got[3]))
        app[:, s, :] = applied
        squares.append(jnp.square(res[:, s, :] - step * applied))
    app_copy = pltpu.make_async_copy(app, applied_out, out_sem.at[1])
    app_copy.start()
    n_row = row_sums(jnp.concatenate(squares, axis=1))
    nn[0] = jnp.concatenate([n_row, n_row], axis=1)

    def n1_copy(k):
        return remote(ex_k(k), nn.at[0], nn.at[k], n1_send.at[k], n1_recv.at[k])

    for k in (10, 9, 11, 6, 14, 8, 2, 5, 7, 13, 15, 1, 3, 4, 12):
        n1_copy(k).start()
    each(NB, lambda k: n1_copy(k).wait())
    nn2[0] = jnp.sum(nn[...], axis=0)

    def n2_copy(k):
        return remote(st_dev(k), nn2.at[0], nn2.at[k], n2_send.at[k], n2_recv.at[k])

    for k in (4, 5, 3, 2, 6, 7, 1):
        n2_copy(k).start()
    both(lambda a, k: d1_copy(a, k).wait_send())
    both(lambda a, k: d2_copy(a, k).wait_send())
    p1_copy().wait_send()
    each(4, lambda k: p2_copy(k).wait_send())

    def i1_sent(far):
        for a in (True, False):
            relay_copy(a, far).wait_send()
            i1_copy(a, 1, far).wait_send()
            i1_copy(a, 3, far).wait_send()

    each(4, i1_sent, 0)
    both(lambda a, k: i2_copy(a, k).wait_send())
    step_copy.wait()
    app_copy.wait()
    each(NS, lambda k: n2_copy(k).wait())
    norm_new = jnp.sum(nn2[...], axis=0)[:, :T]
    conjugacy = column(norm_new / (norm_old + EPSILON))
    for s in range(2):
        wide[1, :, s, :] = jnp.broadcast_to(conjugacy, (T, BLK))
    conj_copy = pltpu.make_async_copy(wide.at[1], conj_out, out_sem.at[2])
    conj_copy.start()
    conj_copy.wait()


def local(embeddings, sign_bits, permutation, gaussian, scaling, phases, solution, residual, direction):
    hbm = pl.BlockSpec(memory_space=pltpu.HBM)
    dma = pltpu.SemaphoreType.DMA
    vmem = pltpu.VMEM
    block, tile = (T, BLK), (8, 128)
    applied, step, conjugacy = pl.pallas_call(
        kernel,
        out_shape=[jax.ShapeDtypeStruct(direction.shape, f32)] * 3,
        in_specs=[hbm] * 8,
        out_specs=[hbm] * 3,
        scratch_shapes=[
            vmem((D, BLK), bf16),
            vmem((2, D), jnp.int32),
            vmem((2, D), f32),
            vmem((2, D), f32),
            vmem((2, D), f32),
            vmem(direction.shape, f32),
            vmem(direction.shape, f32),
            vmem((2, D), jnp.int32),
            vmem((2, D), jnp.int32),
            pltpu.SMEM((D,), jnp.int32),
            pltpu.SMEM((D,), jnp.int32),
            dma((8,)),
            dma((2,)),
            dma((3,)),
            vmem((D, BLK), f32),
            vmem((2 * D, 128), f32),
            vmem((2 * D, 128), f32),
            vmem((2 * D, 128), f32),
            vmem((2 * D, 128), f32),
            vmem((NB, 2 * BLK, BLK), bf16),
            vmem((2, NB, BLK, BLK), bf16),
            vmem((2, NB, BLK, BLK), bf16),
            vmem((D, 8), f32),
            vmem((3, D, 128), f32),
            vmem((3, D, 128), f32),
            vmem((BLK, BLK), f32),
            vmem((BLK, BLK), f32),
            vmem((NB,) + block, f32),
            vmem((NB,) + block, f32),
            vmem((T + 8, BLK), f32),
            vmem((T + 8, BLK), f32),
            vmem((T + 8, BLK), f32),
            vmem((4, T + 8, BLK), f32),
            vmem((4, 4) + block, f32),
            vmem((4, 4) + block, f32),
            vmem((4, 4) + block, f32),
            vmem((4, 4) + block, f32),
            vmem((2, 4) + block, f32),
            vmem((4,) + block, f32),
            vmem((4,) + block, f32),
            vmem((4,) + block, f32),
            vmem((4,) + block, f32),
            vmem(direction.shape, f32),
            vmem((2,) + direction.shape, f32),
            vmem((4, 16, 128), f32),
            vmem((4, 16, 128), f32),
            vmem((NB,) + tile, f32),
            vmem((NS,) + tile, f32),
            dma((2, 4)), dma((2, 4)), dma((2, 4)), dma((2, 4)),
            dma, dma, dma((4,)), dma((4,)),
            dma((2, 4, 4)), dma((2, 4, 4)), dma((2, 4)), dma((2, 4)), dma((2, 4)), dma((2, 4)),
            dma((4,)), dma((4,)), dma((4,)), dma((4,)),
            dma((NB,)), dma((NB,)), dma((NS,)), dma((NS,)),
        ],
        compiler_params=pltpu.CompilerParams(
            collective_id=0, has_side_effects=True, vmem_limit_bytes=60 * 2**20
        ),
    )(embeddings, sign_bits, permutation, gaussian, scaling, phases, residual, direction)
    residual_next = residual - step * applied
    return solution + step * direction, residual_next, residual_next + conjugacy * direction


def solution(mesh):
    rows, stacks, blocks = P(None, "ex"), P("stk", None), P(None, "stk", "ex")
    return jax.shard_map(
        local,
        mesh=mesh,
        in_specs=(rows, stacks, stacks, stacks, stacks, stacks, blocks, blocks, blocks),
        out_specs=(blocks, blocks, blocks),
        check_vma=False,
    )
```

```python
import functools
import math

import jax
import jax.numpy as jnp
from jax import lax
from jax.experimental import pallas as pl
from jax.experimental.pallas import tpu as pltpu
from jax.sharding import PartitionSpec as P

f32, bf16 = jnp.float32, jnp.bfloat16
MESH = pl.DeviceIdType.MESH

D = 4096
BLK = 256
NB = 16
NS = 8
T = 64
RIDGE = 0.25
EPSILON = 1e-06
TURN = 1.0 / (2.0 * math.pi)
NORM = math.sqrt(2.0 / (16 * D))
SINE = (6.283164044251588, -41.337142364570006, 81.34076867837481, -70.99343135659183)
COEF = tuple(c * NORM for c in SINE)


def hadamard():
    i = lax.broadcasted_iota(jnp.int32, (BLK, BLK), 0)
    j = lax.broadcasted_iota(jnp.int32, (BLK, BLK), 1)
    v = i & j
    v = v ^ (v >> 4)
    v = v ^ (v >> 2)
    v = v ^ (v >> 1)
    return (1 - 2 * (v & 1)).astype(f32)


def butterfly(values):
    v = list(values)
    h = 1
    while h < len(v):
        for i in range(0, len(v), 2 * h):
            for k in range(i, i + h):
                v[k], v[k + h] = v[k] + v[k + h], v[k] - v[k + h]
        h *= 2
    return v


def split(x):
    hi = x.astype(bf16)
    return hi, (x - hi.astype(f32)).astype(bf16)


def dot(a, b):
    return jnp.dot(a, b, preferred_element_type=f32)


def dot_t(a, b):
    return lax.dot_general(a, b, (((1,), (1,)), ((), ())), preferred_element_type=f32)


def row_sums(x):
    hi, lo = split(x)
    ones = jnp.ones((8, x.shape[1]), bf16)
    return dot_t(ones, hi) + dot_t(ones, lo)


def column(row):
    wide = jnp.concatenate([row, row], axis=1)
    return jnp.transpose(wide)[:T, 0:1]


def columns_of_parameters(gauss, scale, phase, col):
    for b in range(D // 128):
        at = slice(b * 128, (b + 1) * 128)
        block = jnp.concatenate(
            [
                gauss[:, at],
                scale[:, at] * (TURN / D),
                phase[:, at] * TURN,
                jnp.zeros((2, 128), f32),
            ],
            axis=0,
        )
        col[at, :] = jnp.transpose(block)


def spread_block(s, a, sign, emb, h, y):
    o = pl.multiple_of(a * BLK, BLK)
    signs = (2 * sign[s : s + 1, pl.ds(o, BLK)] - 1).astype(f32)
    y[pl.ds(o, BLK), :] = dot((h * signs).astype(bf16), emb[pl.ds(o, BLK), :])


def spread_across(r, y, sp):
    o = pl.multiple_of(r * 8, 8)
    for half in range(2):
        lanes = slice(half * 128, (half + 1) * 128)
        v = butterfly([y[pl.ds(a * BLK + o, 8), lanes] for a in range(NB)])
        for a in range(NB):
            sp[pl.ds(2 * (a * BLK + o) + half, 8, stride=2), :] = v[a]


def permute(base, rows, perm, sp, yg):
    out = yg.at[pl.ds(pl.multiple_of(2 * base, 2 * 8), 2 * rows)]
    for k in range(rows):
        out[2 * k : 2 * k + 2, :] = sp[pl.ds(perm[base + k], 2), :]


def mix_across(r, yg, bc, z):
    o = pl.multiple_of(r * 16, 16)
    for half in range(2):
        lanes = slice(half * 128, (half + 1) * 128)
        v = butterfly(
            [
                yg[pl.ds(2 * (a * BLK + o) + half, 16, stride=2), :] * bc[0, pl.ds(a * BLK + o, 16), :]
                for a in range(NB)
            ]
        )
        for a in range(NB):
            hi, lo = split(v[a])
            z[a, pl.ds(o, 16), lanes] = hi
            z[a, pl.ds(BLK + o, 16), lanes] = lo


def loop(n, f, unroll=1):
    def body(i, _):
        f(i)
        return 0

    lax.fori_loop(0, n, body, 0, unroll=unroll)


def cosine(turns):
    x = 0.25 - jnp.abs(turns - jnp.round(turns))
    u = x * x
    p = COEF[3]
    for c in COEF[2::-1]:
        p = p * u + c
    return p * x


def spread_parameters(s, a, col, bc):
    at = pl.ds(pl.multiple_of(a * BLK, BLK), BLK)
    for v in range(3):
        bc[v, at, :] = jnp.broadcast_to(col[at, 2 * v + s : 2 * v + s + 1], (BLK, 128))


def features(s, a, ang, bc, fh, fl, also=None):
    o = pl.multiple_of(a * BLK, BLK)
    for c in range(8):
        rows = slice(c * 32, (c + 1) * 32)
        at = pl.ds(o + c * 32, 32)
        for half in range(2):
            lanes = slice(half * 128, (half + 1) * 128)
            hi, lo = split(cosine(ang[rows, lanes] * bc[1, at, :] + bc[2, at, :]))
            fh[s, a, rows, lanes] = hi
            fl[s, a, rows, lanes] = lo
        if also is not None:
            also(c)


def kernel(
    emb_h, sign_h, perm_h, gauss_h, scale_h, phase_h, res_h, dire_h,
    applied_out, step_out, conj_out,
    emb, sign, gauss, scale, phase, res, dire, pv, pv2, perm0, perm1, in_sem, perm_sem, out_sem,
    y, sp, yg, sp1, yg1, z, fh, fl, col, bc0, bc1, ang0, ang1,
    da, db, pacc, psib, pchip, px, sa, sb, ra1, rb1, relay, sa2, sb2, ra2, rb2, app, wide, pp, pp2, nn, nn2,
    d1_send, d1_recv, d2_send, d2_recv,
    p1_send, p1_recv, p2_send, p2_recv, i1_send, i1_recv, i2_send, i2_recv, r_send, r_recv,
    pp_send, pp_recv, pp2_send, pp2_recv, n1_send, n1_recv, n2_send, n2_recv,
):
    ex = lax.axis_index("ex")
    st = lax.axis_index("stk")
    ez, ey = ex // 4, ex % 4

    def ring(i, k):
        return (i + k) % 4

    def ex_dev(dz, dy):
        return (ring(ez, dz) * 4 + ring(ey, dy), st)

    def st_dev(k):
        return (ex, (st + k) % NS)

    sibling = (ex, st + 1 - 2 * (st % 2))

    def remote(dev, src, dst, send, recv):
        return pltpu.make_async_remote_copy(
            src_ref=src, dst_ref=dst, send_sem=send, recv_sem=recv, device_id=dev, device_id_type=MESH
        )

    def each(n, f, first=1, unroll=1):
        def body(k, _):
            f(k)
            return 0

        lax.fori_loop(first, n, body, 0, unroll=unroll)

    def ex_k(k):
        return ex_dev(k // 4, k % 4)

    inputs = [
        pltpu.make_async_copy(src, dst, in_sem.at[i])
        for i, (src, dst) in enumerate(
            [
                (emb_h, emb), (sign_h, sign), (dire_h, dire), (res_h, res), (gauss_h, gauss),
                (scale_h, scale), (phase_h, phase), (perm_h, pv),
            ]
        )
    ]
    for c in inputs:
        c.start()
    barrier = pltpu.get_barrier_semaphore()
    each(NB, lambda k: pl.semaphore_signal(barrier, inc=1, device_id=ex_k(k), device_id_type=MESH))
    each(NS, lambda k: pl.semaphore_signal(barrier, inc=1, device_id=st_dev(k), device_id_type=MESH))

    h = hadamard()
    hb = h.astype(bf16)
    h2 = jnp.concatenate([hb, hb], axis=1)

    inputs[7].wait()
    pv2[...] = 2 * pv[...]
    perm_copies = [
        pltpu.make_async_copy(pv2.at[s], p, perm_sem.at[s]) for s, p in enumerate((perm0, perm1))
    ]
    for c in perm_copies:
        c.start()
    inputs[0].wait()
    inputs[1].wait()
    loop(NB, lambda a: spread_block(0, a, sign, emb, h, y), 4)
    loop(32, lambda r: spread_across(r, y, sp), 2)

    inputs[2].wait()
    inputs[3].wait()
    own_a, own_b = ex, ey * 4 + ez
    da[own_a] = dire[:, 0, :]
    db[own_b] = dire[:, 1, :]

    r2 = row_sums(jnp.concatenate([jnp.square(res[:, s, :]) for s in range(2)], axis=1))
    d2 = row_sums(jnp.concatenate([jnp.square(dire[:, s, :]) for s in range(2)], axis=1))
    pacc[...] = jnp.zeros_like(pacc)
    pacc[T:, :128] = jnp.concatenate([r2, d2], axis=1)

    for i in (4, 5, 6):
        inputs[i].wait()
    for c in perm_copies:
        c.wait()
    columns_of_parameters(gauss, scale, phase, col)

    def permute_spread(i):
        permute(pl.multiple_of(i * 256, 256), 256, perm0, sp, yg)
        for q in range(2):
            spread_block(1, 2 * i + q, sign, emb, h, y)
            spread_parameters(0, 2 * i + q, col, bc0)

    def permute_spread_across(i):
        permute(pl.multiple_of(D // 2 + i * 256, 256), 256, perm0, sp, yg)
        for q in range(4):
            spread_across(4 * i + q, y, sp1)
        for q in range(2):
            spread_parameters(1, 2 * i + q, col, bc1)

    loop(1, permute_spread)
    pl.semaphore_wait(barrier, NB - 1 + NS - 1)
    def d1_copy(a, k):
        if a:
            return remote(ex_dev(0, k), da.at[own_a], da.at[own_a], d1_send.at[0, k], d1_recv.at[0, k])
        return remote(ex_dev(k, 0), db.at[own_b], db.at[own_b], d1_send.at[1, k], d1_recv.at[1, k])

    def d2_copy(a, k):
        four_a, four_b = da.at[pl.ds(ez * 4, 4)], db.at[pl.ds(ey * 4, 4)]
        if a:
            return remote(ex_dev(k, 0), four_a, four_a, d2_send.at[0, k], d2_recv.at[0, k])
        return remote(ex_dev(0, k), four_b, four_b, d2_send.at[1, k], d2_recv.at[1, k])

    def both(f):
        def go(k):
            f(True, k)
            f(False, k)

        each(4, go)

    both(lambda a, k: d1_copy(a, k).start())

    loop(8 - 1, lambda i: permute_spread(1 + i))
    both(lambda a, k: d1_copy(a, k).wait_recv())
    both(lambda a, k: d2_copy(a, k).start())
    loop(8, permute_spread_across)

    def mix_permute(i):
        mix_across(i, yg, bc0, z)
        permute(pl.multiple_of(i * 64, 64), 64, perm1, sp1, yg1)

    def features_permute(j):
        for q in range(2):
            i = 2 * j + q
            features(0, i, (ang0, ang1)[q], bc0, fh, fl)
            permute(pl.multiple_of(16 * 64 + i * 192, 64), 192, perm1, sp1, yg1)
            (ang1, ang0)[q][...] = dot(h2, z[(i + 1) % NB])

    loop(NB, mix_permute)
    ang0[...] = dot(h2, z[0])
    loop(NB // 2, features_permute)

    loop(NB, lambda i: mix_across(i, yg1, bc1, z), 2)

    def project(a):
        part = 0.0
        for s, block in ((0, da[a]), (1, db[(a % 4) * 4 + a // 4])):
            hi, lo = split(block)
            big = dot(jnp.concatenate([hi, lo], axis=0), fh[s, a])
            part += big[:T] + (big[T:] + dot(hi, fl[s, a]))
        pacc[:T] += part

    def features_project(j):
        for q in range(2):
            i = 2 * j + q
            features(1, i, (ang0, ang1)[q], bc1, fh, fl)
            (ang1, ang0)[q][...] = dot(h2, z[(i + 1) % NB])
            project(i)

    ang0[...] = dot(h2, z[0])
    both(lambda a, k: d2_copy(a, k).wait_recv())
    loop(NB // 2, features_project)

    def p1_copy():
        return remote(sibling, pacc, psib, p1_send, p1_recv)

    p1_copy().start()
    p1_copy().wait_recv()
    pchip[...] = pacc[...] + psib[...]

    def p2_copy(k):
        return remote(st_dev(2 * k), pchip, px.at[k], p2_send.at[k], p2_recv.at[k])

    each(4, lambda k: p2_copy(k).start())
    px[0] = pchip[...]
    each(4, lambda k: p2_copy(k).wait_recv())
    summed = (px[0] + px[1]) + (px[2] + px[3])
    projected = summed[:T]
    p_hi, p_lo = split(projected)
    p_both = jnp.concatenate([p_hi, p_lo], axis=0)

    def pp_copy(k):
        return remote(ex_dev(0, k), pp.at[0], pp.at[k], pp_send.at[k], pp_recv.at[k])

    def pp2_copy(k):
        return remote(ex_dev(k, 0), pp2.at[0], pp2.at[k], pp2_send.at[k], pp2_recv.at[k])

    def image(s, e):
        big = dot_t(p_both, fh[s, e])
        return big[:T] + big[T:] + dot_t(p_hi, fl[s, e])

    def i1_copy(a, near, far):
        if a:
            return remote(
                ex_dev(0, near), sa.at[near, far], ra1.at[near, far], i1_send.at[0, near, far], i1_recv.at[0, near, far]
            )
        return remote(
            ex_dev(near, 0), sb.at[near, far], rb1.at[near, far], i1_send.at[1, near, far], i1_recv.at[1, near, far]
        )

    def via(far):
        return 1 + 2 * (far % 2)

    def relay_copy(a, far):
        if a:
            return remote(ex_dev(0, via(far)), sa.at[2, far], relay.at[0, far], r_send.at[0, far], r_recv.at[0, far])
        return remote(ex_dev(via(far), 0), sb.at[2, far], relay.at[1, far], r_send.at[1, far], r_recv.at[1, far])

    def images(near, far):
        sa[near, far] = image(0, ring(ez, far) * 4 + ring(ey, near))
        sb[near, far] = image(1, ring(ez, near) * 4 + ring(ey, far))

    def start_images(near, far):
        i1_copy(True, near, far).start()
        i1_copy(False, near, far).start()

    def opposite(i):
        far = (i + 1) % 4
        images(2, far)
        relay_copy(True, far).start()
        relay_copy(False, far).start()

    def direct(i):
        far = (i + 1) % 4
        images(4 - via(far), far)
        start_images(4 - via(far), far)

    def relayed(i):
        far = (i + 1) % 4
        relay_copy(True, far).wait_recv()
        relay_copy(False, far).wait_recv()
        sa[via(far), far] += relay[0, far]
        sb[via(far), far] += relay[1, far]
        start_images(via(far), far)

    each(4, opposite, 0, 4)

    pp_row = row_sums(jnp.square(projected))
    pp[0, :8] = jnp.concatenate([pp_row, pp_row], axis=1)
    pp[0, 8:] = summed[T:, :128]

    each(4, lambda k: pp_copy(k).start())
    each(4, direct, 0, 4)
    each(4, lambda i: images(via((i + 1) % 4), (i + 1) % 4), 0, 4)
    each(4, relayed, 0)
    each(4, lambda far: images(0, far), 0, 4)

    each(4, lambda k: pp_copy(k).wait())
    pp2[0] = jnp.sum(pp[...], axis=0)
    each(4, lambda k: pp2_copy(k).start())

    def i2_copy(a, k):
        if a:
            return remote(ex_dev(k, 0), sa2.at[k], ra2.at[k], i2_send.at[0, k], i2_recv.at[0, k])
        return remote(ex_dev(0, k), sb2.at[k], rb2.at[k], i2_send.at[1, k], i2_recv.at[1, k])

    def forward(far):
        for a, src, got, out in ((True, sa, ra1, sa2), (False, sb, rb1, sb2)):
            i1_copy(a, 1, far).wait_recv()
            i1_copy(a, 3, far).wait_recv()
            out[far] = src[0, far] + (got[1, far] + got[3, far])

    def forward_out(far):
        forward(far)
        i2_copy(True, far).start()
        i2_copy(False, far).start()

    each(4, forward_out)

    each(4, lambda k: pp2_copy(k).wait())
    totals = jnp.sum(pp2[...], axis=0)
    p_norm, norm_old, d_norm = totals[:8, :T], totals[8:, :T], totals[8:, T:]
    step = column(norm_old / (RIDGE * d_norm + p_norm))
    for s in range(2):
        wide[0, :, s, :] = jnp.broadcast_to(step, (T, BLK))
    step_copy = pltpu.make_async_copy(wide.at[0], step_out, out_sem.at[0])
    step_copy.start()

    forward(0)
    both(lambda a, k: i2_copy(a, k).wait_recv())
    squares = []
    for s, own, got in ((0, sa2, ra2), (1, sb2, rb2)):
        applied = RIDGE * dire[:, s, :] + ((own[0] + got[1]) + (got[2] + got[3]))
        app[:, s, :] = applied
        squares.append(jnp.square(res[:, s, :] - step * applied))
    app_copy = pltpu.make_async_copy(app, applied_out, out_sem.at[1])
    app_copy.start()
    n_row = row_sums(jnp.concatenate(squares, axis=1))
    nn[0] = jnp.concatenate([n_row, n_row], axis=1)

    def n1_copy(k):
        return remote(ex_k(k), nn.at[0], nn.at[k], n1_send.at[k], n1_recv.at[k])

    for k in (10, 9, 11, 6, 14, 8, 2, 5, 7, 13, 15, 1, 3, 4, 12):
        n1_copy(k).start()
    each(NB, lambda k: n1_copy(k).wait())
    nn2[0] = jnp.sum(nn[...], axis=0)

    def n2_copy(k):
        return remote(st_dev(k), nn2.at[0], nn2.at[k], n2_send.at[k], n2_recv.at[k])

    for k in (4, 5, 3, 2, 6, 7, 1):
        n2_copy(k).start()
    both(lambda a, k: d1_copy(a, k).wait_send())
    both(lambda a, k: d2_copy(a, k).wait_send())
    p1_copy().wait_send()
    each(4, lambda k: p2_copy(k).wait_send())

    def i1_sent(far):
        for a in (True, False):
            relay_copy(a, far).wait_send()
            i1_copy(a, 1, far).wait_send()
            i1_copy(a, 3, far).wait_send()

    each(4, i1_sent, 0)
    both(lambda a, k: i2_copy(a, k).wait_send())
    step_copy.wait()
    app_copy.wait()
    each(NS, lambda k: n2_copy(k).wait())
    norm_new = jnp.sum(nn2[...], axis=0)[:, :T]
    conjugacy = column(norm_new / (norm_old + EPSILON))
    for s in range(2):
        wide[1, :, s, :] = jnp.broadcast_to(conjugacy, (T, BLK))
    conj_copy = pltpu.make_async_copy(wide.at[1], conj_out, out_sem.at[2])
    conj_copy.start()
    conj_copy.wait()


def local(embeddings, sign_bits, permutation, gaussian, scaling, phases, solution, residual, direction):
    hbm = pl.BlockSpec(memory_space=pltpu.HBM)
    dma = pltpu.SemaphoreType.DMA
    vmem = pltpu.VMEM
    block, tile = (T, BLK), (8, 128)
    applied, step, conjugacy = pl.pallas_call(
        kernel,
        out_shape=[jax.ShapeDtypeStruct(direction.shape, f32)] * 3,
        in_specs=[hbm] * 8,
        out_specs=[hbm] * 3,
        scratch_shapes=[
            vmem((D, BLK), bf16),
            vmem((2, D), jnp.int32),
            vmem((2, D), f32),
            vmem((2, D), f32),
            vmem((2, D), f32),
            vmem(direction.shape, f32),
            vmem(direction.shape, f32),
            vmem((2, D), jnp.int32),
            vmem((2, D), jnp.int32),
            pltpu.SMEM((D,), jnp.int32),
            pltpu.SMEM((D,), jnp.int32),
            dma((8,)),
            dma((2,)),
            dma((3,)),
            vmem((D, BLK), f32),
            vmem((2 * D, 128), f32),
            vmem((2 * D, 128), f32),
            vmem((2 * D, 128), f32),
            vmem((2 * D, 128), f32),
            vmem((NB, 2 * BLK, BLK), bf16),
            vmem((2, NB, BLK, BLK), bf16),
            vmem((2, NB, BLK, BLK), bf16),
            vmem((D, 8), f32),
            vmem((3, D, 128), f32),
            vmem((3, D, 128), f32),
            vmem((BLK, BLK), f32),
            vmem((BLK, BLK), f32),
            vmem((NB,) + block, f32),
            vmem((NB,) + block, f32),
            vmem((T + 8, BLK), f32),
            vmem((T + 8, BLK), f32),
            vmem((T + 8, BLK), f32),
            vmem((4, T + 8, BLK), f32),
            vmem((4, 4) + block, f32),
            vmem((4, 4) + block, f32),
            vmem((4, 4) + block, f32),
            vmem((4, 4) + block, f32),
            vmem((2, 4) + block, f32),
            vmem((4,) + block, f32),
            vmem((4,) + block, f32),
            vmem((4,) + block, f32),
            vmem((4,) + block, f32),
            vmem(direction.shape, f32),
            vmem((2,) + direction.shape, f32),
            vmem((4, 16, 128), f32),
            vmem((4, 16, 128), f32),
            vmem((NB,) + tile, f32),
            vmem((NS,) + tile, f32),
            dma((2, 4)), dma((2, 4)), dma((2, 4)), dma((2, 4)),
            dma, dma, dma((4,)), dma((4,)),
            dma((2, 4, 4)), dma((2, 4, 4)), dma((2, 4)), dma((2, 4)), dma((2, 4)), dma((2, 4)),
            dma((4,)), dma((4,)), dma((4,)), dma((4,)),
            dma((NB,)), dma((NB,)), dma((NS,)), dma((NS,)),
        ],
        compiler_params=pltpu.CompilerParams(
            collective_id=0, has_side_effects=True, vmem_limit_bytes=60 * 2**20
        ),
    )(embeddings, sign_bits, permutation, gaussian, scaling, phases, residual, direction)
    residual_next = residual - step * applied
    return solution + step * direction, residual_next, residual_next + conjugacy * direction


def solution(mesh):
    rows, stacks, blocks = P(None, "ex"), P("stk", None), P(None, "stk", "ex")
    return jax.shard_map(
        local,
        mesh=mesh,
        in_specs=(rows, stacks, stacks, stacks, stacks, stacks, blocks, blocks, blocks),
        out_specs=(blocks, blocks, blocks),
        check_vma=False,
    )
```

```python
import functools
import math

import jax
import jax.numpy as jnp
from jax import lax
from jax.experimental import pallas as pl
from jax.experimental.pallas import tpu as pltpu
from jax.sharding import PartitionSpec as P

f32, bf16 = jnp.float32, jnp.bfloat16
MESH = pl.DeviceIdType.MESH

D = 4096
BLK = 256
NB = 16
NS = 8
T = 64
RIDGE = 0.25
EPSILON = 1e-06
TURN = 1.0 / (2.0 * math.pi)
NORM = math.sqrt(2.0 / (16 * D))
SINE = (6.283164044251588, -41.337142364570006, 81.34076867837481, -70.99343135659183)
COEF = tuple(c * NORM for c in SINE)


def hadamard():
    i = lax.broadcasted_iota(jnp.int32, (BLK, BLK), 0)
    j = lax.broadcasted_iota(jnp.int32, (BLK, BLK), 1)
    v = i & j
    v = v ^ (v >> 4)
    v = v ^ (v >> 2)
    v = v ^ (v >> 1)
    return (1 - 2 * (v & 1)).astype(f32)


def butterfly(values):
    v = list(values)
    h = 1
    while h < len(v):
        for i in range(0, len(v), 2 * h):
            for k in range(i, i + h):
                v[k], v[k + h] = v[k] + v[k + h], v[k] - v[k + h]
        h *= 2
    return v


def split(x):
    hi = x.astype(bf16)
    return hi, (x - hi.astype(f32)).astype(bf16)


def dot(a, b):
    return jnp.dot(a, b, preferred_element_type=f32)


def dot_t(a, b):
    return lax.dot_general(a, b, (((1,), (1,)), ((), ())), preferred_element_type=f32)


def row_sums(x):
    hi, lo = split(x)
    ones = jnp.ones((8, x.shape[1]), bf16)
    return dot_t(ones, hi) + dot_t(ones, lo)


def column(row):
    wide = jnp.concatenate([row, row], axis=1)
    return jnp.transpose(wide)[:T, 0:1]


def columns_of_parameters(gauss, scale, phase, col):
    for b in range(D // 128):
        at = slice(b * 128, (b + 1) * 128)
        block = jnp.concatenate(
            [
                gauss[:, at],
                scale[:, at] * (TURN / D),
                phase[:, at] * TURN,
                jnp.zeros((2, 128), f32),
            ],
            axis=0,
        )
        col[at, :] = jnp.transpose(block)


def spread_block(s, a, sign, emb, h, y):
    o = pl.multiple_of(a * BLK, BLK)
    signs = (2 * sign[s : s + 1, pl.ds(o, BLK)] - 1).astype(f32)
    y[pl.ds(o, BLK), :] = dot((h * signs).astype(bf16), emb[pl.ds(o, BLK), :])


def spread_across(r, y, sp):
    o = pl.multiple_of(r * 8, 8)
    for half in range(2):
        lanes = slice(half * 128, (half + 1) * 128)
        v = butterfly([y[pl.ds(a * BLK + o, 8), lanes] for a in range(NB)])
        for a in range(NB):
            sp[pl.ds(2 * (a * BLK + o) + half, 8, stride=2), :] = v[a]


def permute(base, rows, perm, sp, yg):
    out = yg.at[pl.ds(pl.multiple_of(2 * base, 2 * 8), 2 * rows)]
    for k in range(rows):
        out[2 * k : 2 * k + 2, :] = sp[pl.ds(perm[base + k], 2), :]


def mix_across(r, yg, bc, z):
    o = pl.multiple_of(r * 16, 16)
    for half in range(2):
        lanes = slice(half * 128, (half + 1) * 128)
        v = butterfly(
            [
                yg[pl.ds(2 * (a * BLK + o) + half, 16, stride=2), :] * bc[0, pl.ds(a * BLK + o, 16), :]
                for a in range(NB)
            ]
        )
        for a in range(NB):
            hi, lo = split(v[a])
            z[a, pl.ds(o, 16), lanes] = hi
            z[a, pl.ds(BLK + o, 16), lanes] = lo


def loop(n, f, unroll=1):
    def body(i, _):
        f(i)
        return 0

    lax.fori_loop(0, n, body, 0, unroll=unroll)


def cosine(turns):
    x = 0.25 - jnp.abs(turns - jnp.round(turns))
    u = x * x
    p = COEF[3]
    for c in COEF[2::-1]:
        p = p * u + c
    return p * x


def spread_parameters(s, a, col, bc):
    at = pl.ds(pl.multiple_of(a * BLK, BLK), BLK)
    for v in range(3):
        bc[v, at, :] = jnp.broadcast_to(col[at, 2 * v + s : 2 * v + s + 1], (BLK, 128))


def features(s, a, ang, bc, fh, fl, also=None):
    o = pl.multiple_of(a * BLK, BLK)
    for c in range(8):
        rows = slice(c * 32, (c + 1) * 32)
        at = pl.ds(o + c * 32, 32)
        for half in range(2):
            lanes = slice(half * 128, (half + 1) * 128)
            hi, lo = split(cosine(ang[rows, lanes] * bc[1, at, :] + bc[2, at, :]))
            fh[s, a, rows, lanes] = hi
            fl[s, a, rows, lanes] = lo
        if also is not None:
            also(c)


def kernel(
    emb_h, sign_h, perm_h, gauss_h, scale_h, phase_h, res_h, dire_h,
    applied_out, step_out, conj_out,
    emb, sign, gauss, scale, phase, res, dire, pv, pv2, perm0, perm1, in_sem, perm_sem, out_sem,
    y, sp, yg, sp1, yg1, z, fh, fl, col, bc0, bc1, ang0, ang1,
    da, db, pacc, psib, pchip, px, sa, sb, ra1, rb1, relay, sa2, sb2, ra2, rb2, app, wide, pp, pp2, nn, nn2,
    d1_send, d1_recv, d2_send, d2_recv,
    p1_send, p1_recv, p2_send, p2_recv, i1_send, i1_recv, i2_send, i2_recv, r_send, r_recv,
    pp_send, pp_recv, pp2_send, pp2_recv, n1_send, n1_recv, n2_send, n2_recv,
):
    ex = lax.axis_index("ex")
    st = lax.axis_index("stk")
    ez, ey = ex // 4, ex % 4

    def ring(i, k):
        return (i + k) % 4

    def ex_dev(dz, dy):
        return (ring(ez, dz) * 4 + ring(ey, dy), st)

    def st_dev(k):
        return (ex, (st + k) % NS)

    sibling = (ex, st + 1 - 2 * (st % 2))

    def remote(dev, src, dst, send, recv):
        return pltpu.make_async_remote_copy(
            src_ref=src, dst_ref=dst, send_sem=send, recv_sem=recv, device_id=dev, device_id_type=MESH
        )

    def each(n, f, first=1, unroll=1):
        def body(k, _):
            f(k)
            return 0

        lax.fori_loop(first, n, body, 0, unroll=unroll)

    def ex_k(k):
        return ex_dev(k // 4, k % 4)

    inputs = [
        pltpu.make_async_copy(src, dst, in_sem.at[i])
        for i, (src, dst) in enumerate(
            [
                (emb_h, emb), (sign_h, sign), (dire_h, dire), (res_h, res), (gauss_h, gauss),
                (scale_h, scale), (phase_h, phase), (perm_h, pv),
            ]
        )
    ]
    for c in inputs:
        c.start()
    barrier = pltpu.get_barrier_semaphore()
    each(NB, lambda k: pl.semaphore_signal(barrier, inc=1, device_id=ex_k(k), device_id_type=MESH))
    each(NS, lambda k: pl.semaphore_signal(barrier, inc=1, device_id=st_dev(k), device_id_type=MESH))

    h = hadamard()
    hb = h.astype(bf16)
    h2 = jnp.concatenate([hb, hb], axis=1)

    inputs[7].wait()
    pv2[...] = 2 * pv[...]
    perm_copies = [
        pltpu.make_async_copy(pv2.at[s], p, perm_sem.at[s]) for s, p in enumerate((perm0, perm1))
    ]
    for c in perm_copies:
        c.start()
    inputs[0].wait()
    inputs[1].wait()
    loop(NB, lambda a: spread_block(0, a, sign, emb, h, y), 4)
    loop(32, lambda r: spread_across(r, y, sp), 2)

    inputs[2].wait()
    inputs[3].wait()
    own_a, own_b = ex, ey * 4 + ez
    da[own_a] = dire[:, 0, :]
    db[own_b] = dire[:, 1, :]

    r2 = row_sums(jnp.concatenate([jnp.square(res[:, s, :]) for s in range(2)], axis=1))
    d2 = row_sums(jnp.concatenate([jnp.square(dire[:, s, :]) for s in range(2)], axis=1))
    pacc[...] = jnp.zeros_like(pacc)
    pacc[T:, :128] = jnp.concatenate([r2, d2], axis=1)

    for i in (4, 5, 6):
        inputs[i].wait()
    for c in perm_copies:
        c.wait()
    columns_of_parameters(gauss, scale, phase, col)

    def permute_spread(i):
        permute(pl.multiple_of(i * 256, 256), 256, perm0, sp, yg)
        for q in range(2):
            spread_block(1, 2 * i + q, sign, emb, h, y)
            spread_parameters(0, 2 * i + q, col, bc0)

    def permute_spread_across(i):
        permute(pl.multiple_of(D // 2 + i * 256, 256), 256, perm0, sp, yg)
        for q in range(4):
            spread_across(4 * i + q, y, sp1)
        for q in range(2):
            spread_parameters(1, 2 * i + q, col, bc1)

    loop(1, permute_spread)
    pl.semaphore_wait(barrier, NB - 1 + NS - 1)
    def d1_copy(a, k):
        if a:
            return remote(ex_dev(0, k), da.at[own_a], da.at[own_a], d1_send.at[0, k], d1_recv.at[0, k])
        return remote(ex_dev(k, 0), db.at[own_b], db.at[own_b], d1_send.at[1, k], d1_recv.at[1, k])

    def d2_copy(a, k):
        four_a, four_b = da.at[pl.ds(ez * 4, 4)], db.at[pl.ds(ey * 4, 4)]
        if a:
            return remote(ex_dev(k, 0), four_a, four_a, d2_send.at[0, k], d2_recv.at[0, k])
        return remote(ex_dev(0, k), four_b, four_b, d2_send.at[1, k], d2_recv.at[1, k])

    def both(f):
        def go(k):
            f(True, k)
            f(False, k)

        each(4, go)

    both(lambda a, k: d1_copy(a, k).start())

    loop(8 - 1, lambda i: permute_spread(1 + i))
    both(lambda a, k: d1_copy(a, k).wait_recv())
    both(lambda a, k: d2_copy(a, k).start())
    loop(8, permute_spread_across)

    def mix_permute(i):
        mix_across(i, yg, bc0, z)
        permute(pl.multiple_of(i * 64, 64), 64, perm1, sp1, yg1)

    def features_permute(j):
        for q in range(2):
            i = 2 * j + q
            features(0, i, (ang0, ang1)[q], bc0, fh, fl)
            permute(pl.multiple_of(16 * 64 + i * 192, 64), 192, perm1, sp1, yg1)
            (ang1, ang0)[q][...] = dot(h2, z[(i + 1) % NB])

    loop(NB, mix_permute, 2)
    ang0[...] = dot(h2, z[0])
    loop(NB // 2, features_permute)

    loop(NB, lambda i: mix_across(i, yg1, bc1, z), 2)

    def project(a):
        part = 0.0
        for s, block in ((0, da[a]), (1, db[(a % 4) * 4 + a // 4])):
            hi, lo = split(block)
            big = dot(jnp.concatenate([hi, lo], axis=0), fh[s, a])
            part += big[:T] + (big[T:] + dot(hi, fl[s, a]))
        pacc[:T] += part

    def features_project(j):
        for q in range(2):
            i = 2 * j + q
            features(1, i, (ang0, ang1)[q], bc1, fh, fl)
            (ang1, ang0)[q][...] = dot(h2, z[(i + 1) % NB])
            project(i)

    ang0[...] = dot(h2, z[0])
    both(lambda a, k: d2_copy(a, k).wait_recv())
    loop(NB // 2, features_project)

    def p1_copy():
        return remote(sibling, pacc, psib, p1_send, p1_recv)

    p1_copy().start()
    p1_copy().wait_recv()
    pchip[...] = pacc[...] + psib[...]

    def p2_copy(k):
        return remote(st_dev(2 * k), pchip, px.at[k], p2_send.at[k], p2_recv.at[k])

    for k in (2, 1, 3):
        p2_copy(k).start()
    px[0] = pchip[...]
    each(4, lambda k: p2_copy(k).wait_recv())
    summed = (px[0] + px[1]) + (px[2] + px[3])
    projected = summed[:T]
    p_hi, p_lo = split(projected)
    p_both = jnp.concatenate([p_hi, p_lo], axis=0)

    def pp_copy(k):
        return remote(ex_dev(0, k), pp.at[0], pp.at[k], pp_send.at[k], pp_recv.at[k])

    def pp2_copy(k):
        return remote(ex_dev(k, 0), pp2.at[0], pp2.at[k], pp2_send.at[k], pp2_recv.at[k])

    def image(s, e):
        big = dot_t(p_both, fh[s, e])
        return big[:T] + big[T:] + dot_t(p_hi, fl[s, e])

    def i1_copy(a, near, far):
        if a:
            return remote(
                ex_dev(0, near), sa.at[near, far], ra1.at[near, far], i1_send.at[0, near, far], i1_recv.at[0, near, far]
            )
        return remote(
            ex_dev(near, 0), sb.at[near, far], rb1.at[near, far], i1_send.at[1, near, far], i1_recv.at[1, near, far]
        )

    def via(far):
        return 1 + 2 * (far % 2)

    def relay_copy(a, far):
        if a:
            return remote(ex_dev(0, via(far)), sa.at[2, far], relay.at[0, far], r_send.at[0, far], r_recv.at[0, far])
        return remote(ex_dev(via(far), 0), sb.at[2, far], relay.at[1, far], r_send.at[1, far], r_recv.at[1, far])

    def images(near, far):
        sa[near, far] = image(0, ring(ez, far) * 4 + ring(ey, near))
        sb[near, far] = image(1, ring(ez, near) * 4 + ring(ey, far))

    def start_images(near, far):
        i1_copy(True, near, far).start()
        i1_copy(False, near, far).start()

    def opposite(i):
        far = (i + 1) % 4
        images(2, far)
        relay_copy(True, far).start()
        relay_copy(False, far).start()

    def direct(i):
        far = (i + 1) % 4
        images(4 - via(far), far)
        start_images(4 - via(far), far)

    def relayed(i):
        far = (i + 1) % 4
        relay_copy(True, far).wait_recv()
        relay_copy(False, far).wait_recv()
        sa[via(far), far] += relay[0, far]
        sb[via(far), far] += relay[1, far]
        start_images(via(far), far)

    each(4, opposite, 0, 4)

    pp_row = row_sums(jnp.square(projected))
    pp[0, :8] = jnp.concatenate([pp_row, pp_row], axis=1)
    pp[0, 8:] = summed[T:, :128]

    each(4, lambda k: pp_copy(k).start())
    each(4, direct, 0, 4)
    each(4, lambda i: images(via((i + 1) % 4), (i + 1) % 4), 0, 4)
    each(4, relayed, 0)
    each(4, lambda far: images(0, far), 0, 4)

    each(4, lambda k: pp_copy(k).wait())
    pp2[0] = jnp.sum(pp[...], axis=0)
    each(4, lambda k: pp2_copy(k).start())

    def i2_copy(a, k):
        if a:
            return remote(ex_dev(k, 0), sa2.at[k], ra2.at[k], i2_send.at[0, k], i2_recv.at[0, k])
        return remote(ex_dev(0, k), sb2.at[k], rb2.at[k], i2_send.at[1, k], i2_recv.at[1, k])

    def forward(far):
        for a, src, got, out in ((True, sa, ra1, sa2), (False, sb, rb1, sb2)):
            i1_copy(a, 1, far).wait_recv()
            i1_copy(a, 3, far).wait_recv()
            out[far] = src[0, far] + (got[1, far] + got[3, far])

    def forward_out(far):
        forward(far)
        i2_copy(True, far).start()
        i2_copy(False, far).start()

    each(4, forward_out)

    each(4, lambda k: pp2_copy(k).wait())
    totals = jnp.sum(pp2[...], axis=0)
    p_norm, norm_old, d_norm = totals[:8, :T], totals[8:, :T], totals[8:, T:]
    step = column(norm_old / (RIDGE * d_norm + p_norm))
    for s in range(2):
        wide[0, :, s, :] = jnp.broadcast_to(step, (T, BLK))
    step_copy = pltpu.make_async_copy(wide.at[0], step_out, out_sem.at[0])
    step_copy.start()

    forward(0)
    both(lambda a, k: i2_copy(a, k).wait_recv())
    squares = []
    for s, own, got in ((0, sa2, ra2), (1, sb2, rb2)):
        applied = RIDGE * dire[:, s, :] + ((own[0] + got[1]) + (got[2] + got[3]))
        app[:, s, :] = applied
        squares.append(jnp.square(res[:, s, :] - step * applied))
    app_copy = pltpu.make_async_copy(app, applied_out, out_sem.at[1])
    app_copy.start()
    n_row = row_sums(jnp.concatenate(squares, axis=1))
    nn[0] = jnp.concatenate([n_row, n_row], axis=1)

    def n1_copy(k):
        return remote(ex_k(k), nn.at[0], nn.at[k], n1_send.at[k], n1_recv.at[k])

    for k in (10, 9, 11, 6, 14, 8, 2, 5, 7, 13, 15, 1, 3, 4, 12):
        n1_copy(k).start()
    each(NB, lambda k: n1_copy(k).wait())
    nn2[0] = jnp.sum(nn[...], axis=0)

    def n2_copy(k):
        return remote(st_dev(k), nn2.at[0], nn2.at[k], n2_send.at[k], n2_recv.at[k])

    for k in (4, 5, 3, 2, 6, 7, 1):
        n2_copy(k).start()
    both(lambda a, k: d1_copy(a, k).wait_send())
    both(lambda a, k: d2_copy(a, k).wait_send())
    p1_copy().wait_send()
    each(4, lambda k: p2_copy(k).wait_send())

    def i1_sent(far):
        for a in (True, False):
            relay_copy(a, far).wait_send()
            i1_copy(a, 1, far).wait_send()
            i1_copy(a, 3, far).wait_send()

    each(4, i1_sent, 0)
    both(lambda a, k: i2_copy(a, k).wait_send())
    step_copy.wait()
    app_copy.wait()
    each(NS, lambda k: n2_copy(k).wait())
    norm_new = jnp.sum(nn2[...], axis=0)[:, :T]
    conjugacy = column(norm_new / (norm_old + EPSILON))
    for s in range(2):
        wide[1, :, s, :] = jnp.broadcast_to(conjugacy, (T, BLK))
    conj_copy = pltpu.make_async_copy(wide.at[1], conj_out, out_sem.at[2])
    conj_copy.start()
    conj_copy.wait()


def local(embeddings, sign_bits, permutation, gaussian, scaling, phases, solution, residual, direction):
    hbm = pl.BlockSpec(memory_space=pltpu.HBM)
    dma = pltpu.SemaphoreType.DMA
    vmem = pltpu.VMEM
    block, tile = (T, BLK), (8, 128)
    applied, step, conjugacy = pl.pallas_call(
        kernel,
        out_shape=[jax.ShapeDtypeStruct(direction.shape, f32)] * 3,
        in_specs=[hbm] * 8,
        out_specs=[hbm] * 3,
        scratch_shapes=[
            vmem((D, BLK), bf16),
            vmem((2, D), jnp.int32),
            vmem((2, D), f32),
            vmem((2, D), f32),
            vmem((2, D), f32),
            vmem(direction.shape, f32),
            vmem(direction.shape, f32),
            vmem((2, D), jnp.int32),
            vmem((2, D), jnp.int32),
            pltpu.SMEM((D,), jnp.int32),
            pltpu.SMEM((D,), jnp.int32),
            dma((8,)),
            dma((2,)),
            dma((3,)),
            vmem((D, BLK), f32),
            vmem((2 * D, 128), f32),
            vmem((2 * D, 128), f32),
            vmem((2 * D, 128), f32),
            vmem((2 * D, 128), f32),
            vmem((NB, 2 * BLK, BLK), bf16),
            vmem((2, NB, BLK, BLK), bf16),
            vmem((2, NB, BLK, BLK), bf16),
            vmem((D, 8), f32),
            vmem((3, D, 128), f32),
            vmem((3, D, 128), f32),
            vmem((BLK, BLK), f32),
            vmem((BLK, BLK), f32),
            vmem((NB,) + block, f32),
            vmem((NB,) + block, f32),
            vmem((T + 8, BLK), f32),
            vmem((T + 8, BLK), f32),
            vmem((T + 8, BLK), f32),
            vmem((4, T + 8, BLK), f32),
            vmem((4, 4) + block, f32),
            vmem((4, 4) + block, f32),
            vmem((4, 4) + block, f32),
            vmem((4, 4) + block, f32),
            vmem((2, 4) + block, f32),
            vmem((4,) + block, f32),
            vmem((4,) + block, f32),
            vmem((4,) + block, f32),
            vmem((4,) + block, f32),
            vmem(direction.shape, f32),
            vmem((2,) + direction.shape, f32),
            vmem((4, 16, 128), f32),
            vmem((4, 16, 128), f32),
            vmem((NB,) + tile, f32),
            vmem((NS,) + tile, f32),
            dma((2, 4)), dma((2, 4)), dma((2, 4)), dma((2, 4)),
            dma, dma, dma((4,)), dma((4,)),
            dma((2, 4, 4)), dma((2, 4, 4)), dma((2, 4)), dma((2, 4)), dma((2, 4)), dma((2, 4)),
            dma((4,)), dma((4,)), dma((4,)), dma((4,)),
            dma((NB,)), dma((NB,)), dma((NS,)), dma((NS,)),
        ],
        compiler_params=pltpu.CompilerParams(
            collective_id=0, has_side_effects=True, vmem_limit_bytes=60 * 2**20
        ),
    )(embeddings, sign_bits, permutation, gaussian, scaling, phases, residual, direction)
    residual_next = residual - step * applied
    return solution + step * direction, residual_next, residual_next + conjugacy * direction


def solution(mesh):
    rows, stacks, blocks = P(None, "ex"), P("stk", None), P(None, "stk", "ex")
    return jax.shard_map(
        local,
        mesh=mesh,
        in_specs=(rows, stacks, stacks, stacks, stacks, stacks, blocks, blocks, blocks),
        out_specs=(blocks, blocks, blocks),
        check_vma=False,
    )
```
